32 devices in a mesh: pool: 4 (over y, x), expert: 8 (over z, core).
Axes of the slice: x: 2, y: 2, z: 4, core: 2. Of those that a mesh axis runs over, the one named last changes fastest.
Arguments:
- queries: bfloat16 [1024, 4096], P(('pool', 'expert')), may hold values from -6 to 6
- kv_cache: bfloat16 [1024, 64, 1024], P(('pool', 'expert')), may hold values from -6 to 6
- block_index: int32 [1024, 8], P(('pool', 'expert')), may hold values from 0 to 31, as said below
- lengths: int32 [1024], P(('pool', 'expert')), may hold values from 2 to 512, as said below
- residual: bfloat16 [1024, 2048], P('pool', 'expert'), may hold values from -21 to 21
- out_weight: bfloat16 [4096, 2048], P(None, 'expert'), may hold values from -0.09375 to 0.09375
- norm_gain: float32 [2048], P('expert'), may hold values from 0.25 to 1.75
- expert_ids: int32 [1024, 8], P('pool'), may hold values from 0 to 31, all different within a row; in each aligned block of 256 rows (0 to 255, 256 to 511, ...) at most 128 rows name the same one
- route_weights: float32 [1024, 8], P('pool'), may hold values from 0.02 to 0.25
- gate_weight: bfloat16 [32, 2048, 768], P(('pool', 'expert')), may hold values from -0.125 to 0.125
- up_weight: bfloat16 [32, 2048, 768], P(('pool', 'expert')), may hold values from -0.125 to 0.125
- down_weight: bfloat16 [32, 768, 2048], P(('pool', 'expert')), may hold values from -0.21875 to 0.21875
Outputs:
- attended: bfloat16 [1024, 2048], P('pool', 'expert')
- expert_mix: bfloat16 [1024, 2048], P('pool', 'expert')
The draws below stay inside these ranges and needn't reach their ends.
Inputs may be any that keep to these rules, and one draw needn't show every extreme that they name: Sequence t reads blocks of the pool of 32 blocks held with it: block (t // 32) * 32 + block_index[t, j] of kv_cache. The first lengths[t] of the sequence's 8 * 64 positions are live. `expert_ids`: each row names 8 different experts; within the 256 rows of one index of pool no expert is named by more than 128 rows.
All inputs are finite; a program needn't handle non-finite values.
Results may differ from the reference program's by a relative error of at most 0.01.
Values may be sent and summed in bfloat16 or wider, within the bound.
No kernel may reach another device: no remote copies, remote signals or barrier semaphores. Data moves between devices by JAX's collectives and lax.ppermute only.
A program may use at most 128 MiB of HBM per device.

```python
import math
import jax
import jax.numpy as jnp
import numpy as np
from jax import lax

D = 2048
HEADS = 32
KV_HEADS = 4
HEAD_DIM = 128
F = 768
TOPK = 8
BLOCK = 64
NBLK = 8
TOK_DEV = 32
BLOCKS_DEV = 32
EXPERTS = 32
TOKENS = 1024
GROUP_ROWS = 256
CAP = 128
BLOCKS = 1024
KVW = 1024
N_POOL = 4


def index_table(key):
    return jax.random.randint(jax.random.fold_in(key, 11), (TOKENS, NBLK), 0, BLOCKS_DEV).astype(jnp.int32)


def draw_block_index(key, part):
    return index_table(key)


def draw_lengths(key, part):
    drawn_lengths = jax.random.randint(jax.random.fold_in(key, 31), (TOKENS,), 2, NBLK * BLOCK + 1)
    row_ids = jnp.arange(TOKENS, dtype=jnp.int32)
    return jnp.where(row_ids % TOK_DEV == 0, NBLK * BLOCK, drawn_lengths).astype(jnp.int32)


def draw_queries(key, part):
    normal_part = jnp.clip(jax.random.normal(jax.random.fold_in(key, 41), (TOKENS, HEADS, HEAD_DIM), jnp.float32), -6.0, 6.0)
    return normal_part.reshape(TOKENS, HEADS * HEAD_DIM).astype(jnp.bfloat16)


def draw_kv_cache(key, part):
    normal_part = jnp.clip(jax.random.normal(jax.random.fold_in(key, 51), (BLOCKS, BLOCK, KVW), jnp.float32), -6.0, 6.0)
    return normal_part.astype(jnp.bfloat16)


def draw_residual(key, part):
    column_pos = jnp.arange(D, dtype=jnp.float32) / (D - 1)
    noise = jnp.clip(jax.random.normal(jax.random.fold_in(key, 64), (TOKENS, D), jnp.float32), -6.0, 6.0)
    return (noise * 0.5 * jnp.exp(math.log(3.0) * column_pos)[None, :]).astype(jnp.bfloat16)


def block_scale(key, shape, split, smallest, largest):
    gain, own = 1.0, jax.random.fold_in(key, 6)
    for axis_at, shards_of in split:
        heights = jnp.exp(jax.random.uniform(jax.random.fold_in(own, axis_at), (shards_of,), jnp.float32, smallest / len(split), largest / len(split)))
        gain = gain * jnp.repeat(heights, shape[axis_at] // shards_of).reshape([-1 if axis == axis_at else 1 for axis in range(len(shape))])
    return gain


def shared_out(stream_key, own, number, rows, number_of, top, most, skew):
    sequence = jax.random.permutation(stream_key, number_of)
    heavy_load, common = load_shares(number_of, rows * top, most, skew, True), load_shares(number_of, rows * top, most, skew, False)
    places = jnp.arange(number_of)

    def named(tallies, rotation):
        used = int((tallies > 0).sum())
        fixed = max(1, used // 4)
        shifted = fixed + (places - fixed + rotation * (used - fixed)) % max(1, number_of - fixed)
        return jnp.zeros((number_of,), jnp.int32).at[sequence[jnp.where(places < fixed, places, shifted)]].set(jnp.asarray(tallies, jnp.int32))

    tallies = jnp.where(number % 4 == 0, named(heavy_load, number // 4), named(common, number - number // 4 - 1))
    mixed = jax.random.permutation(jax.random.fold_in(own, 3), number_of)
    source_of, receiver = mixed[0:number_of // 2 * 2:2], mixed[1:number_of // 2 * 2:2]
    margin = jnp.minimum(tallies[source_of] - 1, most - tallies[receiver]) // 2
    margin = jnp.where((source_of == sequence[0]) | (receiver == sequence[0]) | (tallies[receiver] == 0), 0, jnp.maximum(margin, 0))
    shifted = jax.random.randint(jax.random.fold_in(own, 4), (number_of // 2,), 0, 1 << 20) % (margin + 1)
    tallies = tallies.at[source_of].add(-shifted).at[receiver].add(shifted)
    members = jnp.searchsorted(jnp.cumsum(tallies), jnp.arange(rows * top), side="right").astype(jnp.int32)
    grid = members.reshape(top, rows).T
    grid = grid[jax.random.permutation(jax.random.fold_in(own, 1), rows)]
    rotation = jax.random.randint(jax.random.fold_in(own, 2), (rows, 1), 0, top)
    return jnp.take_along_axis(grid, (jnp.arange(top)[None, :] + rotation) % top, axis=1)


def load_shares(number_of, total, limit, skew, full):
    loads = [(1 << 20) // math.isqrt(rank ** skew) + 1 for rank in range(1, number_of + 1)]
    largest = limit if full else min(limit, max(-(-total // number_of), total * loads[0] // sum(loads)))
    least = 1 if total - largest >= number_of - 1 else 0
    holding, surplus = [largest] + [least] * (number_of - 1), total - largest - least * (number_of - 1)
    while surplus > 0:
        free = [i for i in range(1, number_of) if holding[i] < largest] or [i for i in range(1, number_of) if holding[i] < limit]
        mass, budget = sum([loads[i] for i in free]), surplus
        for i in free:
            extra = min(limit - holding[i], max(1, budget * loads[i] // mass), surplus)
            holding[i] = holding[i] + extra
            surplus = surplus - extra
    return np.array(holding)


def gaussian(own_key, extent, width, limit, split=(), kind=jnp.bfloat16):
    drawn = width * jax.random.normal(own_key, extent, jnp.float32)
    if split:
        drawn = drawn * block_scale(own_key, extent, split, -0.22, 0.18)
    return jnp.clip(drawn, -limit, limit).astype(kind)


def setup_inputs(seed: int = 0) -> dict:
    streams_of = jax.random.split(jax.random.key(seed), 13)
    queries = draw_queries(jax.random.fold_in(streams_of[12], 71), 0)
    kv_cache = draw_kv_cache(jax.random.fold_in(streams_of[12], 71), 0)
    block_index = draw_block_index(jax.random.fold_in(streams_of[12], 71), 0)
    lengths = draw_lengths(jax.random.fold_in(streams_of[12], 71), 0)
    residual = draw_residual(jax.random.fold_in(streams_of[12], 71), 0)
    out_weight = gaussian(streams_of[5], (HEADS * HEAD_DIM, D), (HEADS * HEAD_DIM) ** -0.5, 0.09375, ((1, 8),))
    norm_gain = jnp.clip(1.0 + 0.15 * jax.random.normal(streams_of[6], (D,), jnp.float32), 0.25, 1.75)
    expert_ids_keys = jax.random.split(jax.random.fold_in(streams_of[7], 1), TOKENS // GROUP_ROWS)
    expert_ids_turns = jax.random.permutation(jax.random.fold_in(streams_of[7], 3), TOKENS // GROUP_ROWS)
    expert_ids = jax.vmap(lambda own, number: shared_out(jax.random.fold_in(streams_of[7], 2), own, number, GROUP_ROWS, EXPERTS, TOPK, CAP, 2))(expert_ids_keys, expert_ids_turns).reshape((TOKENS, TOPK))
    route_weights = jnp.clip(0.02 + 0.23 * jax.random.uniform(streams_of[8], (TOKENS, TOPK), jnp.float32) ** block_scale(streams_of[8], (TOKENS, TOPK), ((0, 4),), -0.2, 0.2), 0.02, 0.25)
    gate_weight = gaussian(streams_of[9], (EXPERTS, D, F), D ** -0.5, 0.125, ((0, 32),))
    up_weight = gaussian(streams_of[10], (EXPERTS, D, F), D ** -0.5, 0.125, ((0, 32),))
    down_weight = gaussian(streams_of[11], (EXPERTS, F, D), F ** -0.5, 0.21875, ((0, 32),))
    return dict(queries=queries, kv_cache=kv_cache, block_index=block_index, lengths=lengths, residual=residual, out_weight=out_weight, norm_gain=norm_gain, expert_ids=expert_ids, route_weights=route_weights, gate_weight=gate_weight, up_weight=up_weight, down_weight=down_weight)


epsilon = 1e-06

def attend_rows(queries, kv_cache, block_index, lengths):
    context = NBLK * BLOCK
    half_width = KV_HEADS * HEAD_DIM
    group_size = HEADS // KV_HEADS
    owners = jnp.arange(TOKENS, dtype=jnp.int32) // TOK_DEV * BLOCKS_DEV
    global_blocks = (block_index + owners[:, None]).astype(jnp.int32)
    positions = jnp.arange(context, dtype=jnp.int32)

    def one_row(inputs):
        query_row, blocks_row, length_row = inputs
        gathered = kv_cache[blocks_row].reshape(context, 2 * half_width)
        key_part = gathered[:, :half_width].reshape(context, KV_HEADS, HEAD_DIM).astype(jnp.float32)
        value_part = gathered[:, half_width:].reshape(context, KV_HEADS, HEAD_DIM).astype(jnp.float32)
        query_split = query_row.reshape(KV_HEADS, group_size, HEAD_DIM).astype(jnp.float32)
        scores = jnp.einsum('gqd,pgd->gqp', query_split, key_part) * HEAD_DIM ** (-0.5)
        live_mask = positions < length_row
        scores = jnp.where(live_mask[None, None, :], scores, -1e+30)
        maximum = lax.optimization_barrier(jnp.max(scores, axis=-1, keepdims=True))
        exponent = jnp.exp(scores - maximum)
        softmax_w = (exponent / lax.optimization_barrier(jnp.sum(exponent, axis=-1, keepdims=True))).astype(jnp.bfloat16)
        attended_part = jnp.einsum('gqp,pgd->gqd', softmax_w.astype(jnp.float32), value_part)
        return attended_part.astype(jnp.bfloat16).reshape(HEADS * HEAD_DIM)
    return lax.map(one_row, (queries, global_blocks, lengths))

def expert_ffn(inputs):
    rows_in, gate_w, up_w, down_w = inputs
    gate_act = jnp.dot(rows_in, gate_w, preferred_element_type=jnp.float32)
    upper = jnp.dot(rows_in, up_w, preferred_element_type=jnp.float32)
    hidden = (jax.nn.silu(gate_act) * upper).astype(jnp.bfloat16)
    return jnp.dot(hidden, down_w, preferred_element_type=jnp.float32).astype(jnp.bfloat16)

def reference(queries, kv_cache, block_index, lengths, residual, out_weight, norm_gain, expert_ids, route_weights, gate_weight, up_weight, down_weight):
    attention = attend_rows(queries, kv_cache, block_index, lengths)
    projected = jnp.dot(attention, out_weight, preferred_element_type=jnp.float32)
    attended = (residual.astype(jnp.float32) + projected).astype(jnp.bfloat16)
    attended_f = attended.astype(jnp.float32)
    square_sum = lax.optimization_barrier(jnp.sum(attended_f * attended_f, axis=1, keepdims=True))
    normed = (attended_f * lax.rsqrt(square_sum / D + epsilon) * norm_gain[None, :]).astype(jnp.bfloat16)
    flat_ids = expert_ids.reshape(N_POOL, GROUP_ROWS * TOPK)
    onehot = (flat_ids[:, :, None] == jnp.arange(EXPERTS, dtype=jnp.int32)[None, None, :]).astype(jnp.int32)
    before = jnp.cumsum(onehot, axis=1) - onehot
    slot_ids = lax.optimization_barrier(jnp.sum(before * onehot, axis=2)).astype(jnp.int32)
    row_place = (jnp.arange(N_POOL, dtype=jnp.int32)[:, None] * CAP + slot_ids).reshape(-1)
    expert_flat = flat_ids.reshape(-1)
    sources = jnp.repeat(normed, TOPK, axis=0)
    buffers = jnp.zeros((EXPERTS, N_POOL * CAP, D), jnp.bfloat16).at[expert_flat, row_place].set(sources)
    expert_out = lax.map(expert_ffn, (buffers, gate_weight, up_weight, down_weight))
    picked = expert_out[expert_flat, row_place].reshape(TOKENS, TOPK, D).astype(jnp.float32)
    expert_mix = lax.optimization_barrier(jnp.sum(picked * route_weights[:, :, None], axis=1)).astype(jnp.bfloat16)
    return (attended, expert_mix)
```

```python
import functools
import math

import jax
import jax.numpy as jnp
from jax import lax
from jax.experimental import pallas as pl
from jax.experimental.pallas import tpu as pltpu
from jax.sharding import PartitionSpec as P

HEAD_DIM = 128
CORES = 2
MASKED = -1e30
GAIN_COLUMNS = 128
TURN_ROWS = 16
ID_COLUMNS = 128
LARGE_VMEM = 60 * 2**20
SMALL_VMEM = 24 * 2**20
FETCH_VMEM = 46 * 2**20

epsilon = 1e-06


def prepare(residual_ref, gain_ref, out_ref, columns_ref):
    member = lax.axis_index("expert")
    core = member - member // CORES * CORES
    line = lax.axis_size("expert") // CORES
    rows = out_ref.shape[0] // line
    for z in range(line):
        at = pl.ds(pl.multiple_of((z * CORES + 1 - core) * rows, rows), rows)
        out_ref[z * rows : (z + 1) * rows, :] = residual_ref[at, :]
    lines = [
        term[:, at : at + GAIN_COLUMNS]
        for term in three_terms(gain_ref[...])
        for at in range(0, gain_ref.shape[1], GAIN_COLUMNS)
    ]
    lines.append(jnp.zeros((columns_ref.shape[0] - len(lines), GAIN_COLUMNS), jnp.float32))
    columns_ref[...] = jnp.concatenate(lines, axis=0).astype(jnp.bfloat16)


def attend_kernel(index_ref, length_ref, query_ref, kv_hbm, *refs, block_len, first, prepares):
    if prepares:
        residual_ref, gain_ref, out_ref, extra_ref, bias_ref, key_ref, value_ref, sems = refs
    else:
        out_ref, bias_ref, key_ref, value_ref, sems = refs
    blocks_row, rows = index_ref.shape
    positions, width = key_ref.shape
    heads = width // HEAD_DIM
    kv_half = kv_hbm.shape[1] // 2
    group_size = query_ref.shape[1] // heads // HEAD_DIM
    scale = HEAD_DIM ** (-0.5)
    base2 = scale * math.log2(math.e)
    pieces = sems.shape[1]
    copies = []
    for kind, (start, target) in enumerate(((0, key_ref), (kv_half, value_ref))):
        columns = pl.ds(start + first * HEAD_DIM, width)
        for piece in range(pieces):
            at = pl.ds(piece * (positions // pieces), positions // pieces)
            copies.append(
                pltpu.make_async_copy(
                    kv_hbm.at[at, columns], target.at[at, :], sems.at[kind, piece]
                )
            )
    for copy in copies[:pieces]:
        copy.start()
    if prepares:
        columns_ref = out_ref.at[:, pl.ds(query_ref.shape[1], GAIN_COLUMNS)]
        prepare(residual_ref, gain_ref, extra_ref, columns_ref)

    length = length_ref[...].astype(jnp.float32)
    high = jnp.floor(length * (1.0 / 16)) * 16.0
    pad = jnp.zeros((TURN_ROWS - blocks_row - 2, rows), jnp.float32)
    table = jnp.concatenate(
        [
            index_ref[...].astype(jnp.float32),
            high,
            length - high,
            pad,
        ],
        axis=0,
    ).astype(jnp.bfloat16)
    same = lax.broadcasted_iota(jnp.int32, (rows, rows), 0) == lax.broadcasted_iota(
        jnp.int32, (rows, rows), 1
    )
    table = lax.dot_general(
        same.astype(jnp.float32).astype(jnp.bfloat16),
        table,
        (((1,), (1,)), ((), ())),
        preferred_element_type=jnp.float32,
    )
    limit = table[:, blocks_row : blocks_row + 1] + table[:, blocks_row + 1 : blocks_row + 2]
    place = lax.broadcasted_iota(jnp.int32, (rows, positions), 1).astype(jnp.float32)
    block = jnp.floor((place + 0.5) * (1.0 / block_len))
    offset = place - block * block_len
    count = jnp.zeros((rows, positions), jnp.float32)
    for j in range(blocks_row):
        live = (table[:, j : j + 1] == block) & (offset < limit - j * block_len)
        count = count + jnp.where(live, 1.0, 0.0)
    bias_ref[...] = jnp.where(
        count > 0.0, jnp.log(jnp.maximum(count, 1.0)) * (1.0 / scale), MASKED
    )

    for g in range(heads):
        columns = [
            slice((g * group_size + h) * HEAD_DIM, (g * group_size + h + 1) * HEAD_DIM)
            for h in range(group_size)
        ]
        head = slice(g * HEAD_DIM, (g + 1) * HEAD_DIM)
        query = jnp.concatenate([query_ref[:, at] for at in columns], axis=0)
        if g == 0:
            for copy in copies[:pieces]:
                copy.wait()
            for copy in copies[pieces:]:
                copy.start()
        scores = lax.dot_general(
            query, key_ref[:, head], (((1,), (1,)), ((), ())), preferred_element_type=jnp.float32
        )
        scores = scores.reshape(group_size, rows, positions) + bias_ref[...][None]
        maximum = jnp.max(scores, axis=-1, keepdims=True)
        exponent = jnp.exp2((scores - maximum) * base2)
        total = jnp.sum(exponent, axis=-1, keepdims=True)
        weights = exponent.astype(jnp.bfloat16).reshape(group_size * rows, positions)
        if g == 0:
            for copy in copies[pieces:]:
                copy.wait()
        mixed = jnp.dot(weights, value_ref[:, head], preferred_element_type=jnp.float32)
        mixed = mixed.reshape(group_size, rows, HEAD_DIM) / total
        for h, at in enumerate(columns):
            out_ref[:, at] = mixed[h].astype(jnp.bfloat16)


def attend(queries, kv_cache, block_index, lengths, part, parts, prepared=None):
    rows = queries.shape[0]
    pool_blocks, block_len, kv_width = kv_cache.shape
    positions = pool_blocks * block_len
    kv_heads = kv_width // 2 // HEAD_DIM
    width = queries.shape[1] // kv_heads
    kv_flat = kv_cache.reshape(positions, kv_width)
    heads = kv_heads // parts
    first = part * heads
    operands = []
    columns = 0 if prepared is None else GAIN_COLUMNS
    out_shape = [pltpu.VMEM((rows, heads * width + columns), jnp.bfloat16)]
    if prepared is not None:
        residual, gain = prepared
        operands = [residual, gain.reshape(1, -1)]
        extra = (residual.shape[0] // CORES, residual.shape[1])
        out_shape.append(pltpu.VMEM(extra, jnp.bfloat16))
    return pl.pallas_call(
        functools.partial(
            attend_kernel, block_len=block_len, first=first, prepares=prepared is not None
        ),
        grid=(1,),
        in_specs=[
            pl.BlockSpec((block_index.shape[1], rows), lambda g: (0, 0)),
            pl.BlockSpec((1, rows), lambda g: (0, 0)),
            pl.BlockSpec((rows, heads * width), lambda g: (0, part)),
            pl.BlockSpec(memory_space=pl.ANY),
        ]
        + [pl.BlockSpec(operand.shape, lambda g: (0, 0)) for operand in operands],
        out_specs=[pl.BlockSpec(shape.shape, lambda g: (0, 0)) for shape in out_shape],
        out_shape=out_shape,
        scratch_shapes=[
            pltpu.VMEM((rows, positions), jnp.float32),
            pltpu.VMEM((positions, heads * HEAD_DIM), jnp.bfloat16),
            pltpu.VMEM((positions, heads * HEAD_DIM), jnp.bfloat16),
            pltpu.SemaphoreType.DMA((2, 2)),
        ],
        compiler_params=pltpu.CompilerParams(vmem_limit_bytes=LARGE_VMEM),
        name="attend",
    )(block_index.T, lengths.reshape(1, rows), queries, kv_flat, *operands)


def fetch_kernel(*refs, count):
    sems = refs[2 * count]
    copies = [
        pltpu.make_async_copy(refs[i], refs[count + i], sems.at[i]) for i in range(count)
    ]
    for copy in copies:
        copy.start()
    for copy in copies:
        copy.wait()


def fetch(*arrays):
    count = len(arrays)
    return pl.pallas_call(
        functools.partial(fetch_kernel, count=count),
        in_specs=[pl.BlockSpec(memory_space=pltpu.HBM)] * count,
        out_specs=[pl.BlockSpec(memory_space=pltpu.VMEM)] * count,
        out_shape=[pltpu.VMEM(array.shape, array.dtype) for array in arrays],
        scratch_shapes=[pltpu.SemaphoreType.DMA((count,))],
        compiler_params=pltpu.CompilerParams(vmem_limit_bytes=FETCH_VMEM),
        cost_estimate=pl.CostEstimate(
            flops=0, transcendentals=0, bytes_accessed=2 * sum(a.size * 2 for a in arrays)
        ),
        name="fetch",
    )(*arrays)


def project_kernel(*refs, line, parts):
    blocks = refs[: line * parts]
    (
        weight_ref,
        other_weight_ref,
        residual_ref,
        extra_ref,
        message_ref,
        mine_ref,
        give_ref,
    ) = refs[line * parts :]
    rows = blocks[0].shape[0]
    core_rows = line * rows
    width = weight_ref.shape[1]
    member = lax.axis_index("expert")
    layer = member // CORES
    core = member - layer * CORES
    depth = blocks[-1].shape[1]
    product = other_product = 0.0
    for part in range(parts):
        gathered = [ref[:, :depth] for ref in blocks[part * line : (part + 1) * line]]
        gathered = jnp.concatenate(gathered, axis=0)
        at = slice(part * depth, (part + 1) * depth)
        product += jnp.dot(gathered, weight_ref[at, :], preferred_element_type=jnp.float32)
        other_product += jnp.dot(
            gathered, other_weight_ref[at, :], preferred_element_type=jnp.float32
        )
    here = pl.ds(pl.multiple_of(core * width, width), width)
    there = pl.ds(pl.multiple_of((1 - core) * width, width), width)
    for k in range(line):
        z = layer - k
        z = jnp.where(z < 0, z + line, z)
        at = pl.ds(pl.multiple_of(z * rows, rows), rows)
        held = pl.ds(pl.multiple_of((z * CORES + core) * rows, rows), rows)
        arrived = slice(k * rows, (k + 1) * rows)
        mine = residual_ref[held, :].astype(jnp.float32) + product[arrived, :]
        mine = mine.astype(jnp.bfloat16)
        mine_ref[at, :] = mine
        message_ref[at, here] = mine
        other = extra_ref[at, :].astype(jnp.float32) + other_product[arrived, :]
        other = other.astype(jnp.bfloat16)
        give_ref[at, :] = other
        message_ref[at, there] = other
    gains = []
    pieces = width // GAIN_COLUMNS
    for k in range(line):
        lines = blocks[k][:16, depth:].astype(jnp.float32)
        for term in range(3):
            gains.append(
                jnp.concatenate(
                    [lines[term * pieces + p : term * pieces + p + 1] for p in range(pieces)], axis=1
                )
            )
    gains.append(jnp.zeros((give_ref.shape[0] - core_rows - len(gains), width), jnp.float32))
    give_ref[core_rows:, :] = jnp.concatenate(gains, axis=0).astype(jnp.bfloat16)


def project(blocks, weight, other_weight, residual, extra, parts):
    line = len(blocks) // parts
    core_rows = blocks[0].shape[0] * line
    width = weight.shape[1]
    vmem = pl.BlockSpec(memory_space=pltpu.VMEM)
    return pl.pallas_call(
        functools.partial(project_kernel, line=line, parts=parts),
        in_specs=[vmem] * (line * parts + 4),
        out_specs=[vmem] * 3,
        out_shape=[
            jax.ShapeDtypeStruct((core_rows, CORES * width), jnp.bfloat16),
            jax.ShapeDtypeStruct((core_rows, width), jnp.bfloat16),
            jax.ShapeDtypeStruct((core_rows + pl.cdiv(3 * line, 16) * 16, width), jnp.bfloat16),
        ],
        compiler_params=pltpu.CompilerParams(vmem_limit_bytes=SMALL_VMEM),
        name="project",
    )(*blocks, weight, other_weight, residual, extra)


def three_terms(value):
    terms = []
    for _ in range(3):
        terms.append(value.astype(jnp.bfloat16).astype(jnp.float32))
        value = value - terms[-1]
    return terms


def lines_kernel(ids_ref, route_ref, out_ref, *chosen, line):
    core_rows = out_ref.shape[0]
    top_count, group_rows = ids_ref.shape
    rows = group_rows // (line * CORES)
    lines = []
    terms = [ids_ref[...].astype(jnp.float32), *three_terms(route_ref[...])]
    for value in terms:
        value = jnp.concatenate(
            [
                value[:, (z * CORES + c) * rows : (z * CORES + c + 1) * rows]
                for c in range(CORES)
                for z in range(line)
            ],
            axis=1,
        )
        lines += [value[:, at : at + ID_COLUMNS] for at in range(0, group_rows, ID_COLUMNS)]
    used = top_count * len(lines)
    if used < core_rows:
        lines.append(jnp.zeros((core_rows - used, ID_COLUMNS), jnp.float32))
    out_ref[...] = jnp.concatenate(lines, axis=0).astype(jnp.bfloat16)
    pool = lax.axis_index("pool")
    member = lax.axis_index("expert")
    core = member - member // CORES * CORES
    owners = []
    for j in range(len(chosen)):
        step = pair_step(lax.axis_size("pool"), j, core)
        owners.append((pool ^ step) * lax.axis_size("expert") + member)
    for ref, matrix in zip(chosen, plan(terms, owners, chosen[0].shape[1], line)):
        ref[...] = matrix


def routing_lines(ids, route_weights, line, near_count, capacity):
    vmem = pl.BlockSpec(memory_space=pltpu.VMEM)
    return pl.pallas_call(
        functools.partial(lines_kernel, line=line),
        in_specs=[vmem] * 2,
        out_specs=[vmem] * (1 + near_count),
        out_shape=[jax.ShapeDtypeStruct((ids.shape[1] // CORES, ID_COLUMNS), jnp.bfloat16)]
        + [jax.ShapeDtypeStruct((ids.shape[1], capacity), jnp.bfloat16)] * near_count,
        compiler_params=pltpu.CompilerParams(vmem_limit_bytes=SMALL_VMEM),
        name="lines",
    )(ids, route_weights)


def normalize_kernel(lines_ref, give_ref, taken_ref, *refs):
    blocks = refs[:-1]
    out_ref = refs[-1]
    line = len(blocks)
    width = blocks[0].shape[1]
    core_rows = out_ref.shape[0]
    features = line * width
    member = lax.axis_index("expert")
    layer = member // CORES
    core = member - layer * CORES
    gains = [ref[core_rows:, :].astype(jnp.float32) for ref in (give_ref, taken_ref)]
    squares = jnp.zeros((core_rows, 1), jnp.float32)
    for block in blocks:
        attended = block[...].astype(jnp.float32)
        squares = squares + jnp.sum(attended * attended, axis=1, keepdims=True)
    inverse = lax.rsqrt(squares / features + epsilon)
    for k, block in enumerate(blocks):
        z = layer - k
        z = jnp.where(z < 0, z + line, z)
        at = pl.ds(pl.multiple_of(z * width, width), width)
        attended = block[...].astype(jnp.float32)
        mine, other = [jnp.sum(gain[3 * k : 3 * k + 3], axis=0, keepdims=True) for gain in gains]
        gain = jnp.where(
            core == 0,
            jnp.concatenate([mine, other], axis=1),
            jnp.concatenate([other, mine], axis=1),
        )
        out_ref[:, at] = (attended * inverse * gain).astype(jnp.bfloat16)

    out_ref[:, features:] = lines_ref[...]


def assemble_kernel(mine_ref, taken_ref, out_ref, *, line):
    rows = mine_ref.shape[0] // line
    member = lax.axis_index("expert")
    core = member - member // CORES * CORES
    for z in range(line):
        at = slice(z * rows, (z + 1) * rows)
        here = pl.ds(pl.multiple_of((z * CORES + core) * rows, rows), rows)
        there = pl.ds(pl.multiple_of((z * CORES + 1 - core) * rows, rows), rows)
        out_ref[here, :] = mine_ref[at, :]
        out_ref[there, :] = taken_ref[at, :]


def assemble(mine, taken, line):
    vmem = pl.BlockSpec(memory_space=pltpu.VMEM)
    return pl.pallas_call(
        functools.partial(assemble_kernel, line=line),
        in_specs=[vmem] * 2,
        out_specs=vmem,
        out_shape=jax.ShapeDtypeStruct((CORES * mine.shape[0], mine.shape[1]), mine.dtype),
        compiler_params=pltpu.CompilerParams(vmem_limit_bytes=SMALL_VMEM),
        name="assemble",
    )(mine, taken)


def normalize(blocks, lines, give, taken):
    rows, width = blocks[0].shape
    features = len(blocks) * width
    vmem = pl.BlockSpec(memory_space=pltpu.VMEM)
    return pl.pallas_call(
        normalize_kernel,
        in_specs=[vmem] * (len(blocks) + 3),
        out_specs=vmem,
        out_shape=jax.ShapeDtypeStruct((rows, features + ID_COLUMNS), jnp.bfloat16),
        compiler_params=pltpu.CompilerParams(vmem_limit_bytes=SMALL_VMEM),
        name="normalize",
    )(lines, give, taken, *blocks)


def routing(rows_ref, features, top_count, kinds):
    group_rows = CORES * rows_ref.shape[0]
    pieces = group_rows // ID_COLUMNS
    lines = rows_ref[: kinds * top_count * pieces, features:].astype(jnp.float32)
    found = []
    for kind in range(kinds):
        first = kind * pieces * top_count
        found.append(
            jnp.concatenate(
                [lines[first + p * top_count : first + (p + 1) * top_count] for p in range(pieces)],
                axis=1,
            )
        )
    return found


def expert_kernel(*refs, count, top_count, line, parts):
    inputs = [(refs[2 * i], refs[2 * i + 1]) for i in range(count)]
    gate_ref, up_ref, down_ref = refs[2 * count : 2 * count + 3]
    outs = refs[2 * count + 3 :]
    capacity = outs[0].shape[0]
    features = gate_ref.shape[1]
    width = features // (CORES * line)
    pool = lax.axis_index("pool")
    member = lax.axis_index("expert")
    layer = member // CORES
    core = member - layer * CORES
    owner = (pool * lax.axis_size("expert") + member).astype(jnp.float32)

    half = inputs[0][0].shape[0]
    group_rows = CORES * half
    before = (
        lax.broadcasted_iota(jnp.int32, (group_rows, group_rows), 0)
        < lax.broadcasted_iota(jnp.int32, (group_rows, group_rows), 1)
    ).astype(jnp.bfloat16)
    slots = lax.broadcasted_iota(jnp.int32, (capacity, group_rows), 0)
    rows = []
    for mine_ref, other_ref in inputs:
        (ids,) = routing(mine_ref, features, top_count, 1)
        routed = jnp.max((ids == owner).astype(jnp.float32), axis=0, keepdims=True)
        mask = jnp.broadcast_to(routed, (16, group_rows)).astype(jnp.bfloat16)
        slot = jnp.dot(mask, before, preferred_element_type=jnp.float32)[0:1, :]
        slot = jnp.where(routed > 0.0, slot, -1.0).astype(jnp.int32)
        chosen = (slot == slots).astype(jnp.float32)
        first, second = chosen[:, :half], chosen[:, half:]
        mine = jnp.where(core == 0, first, second).astype(jnp.bfloat16)
        other = jnp.where(core == 0, second, first).astype(jnp.bfloat16)
        picked = jnp.dot(mine, mine_ref[:, :features], preferred_element_type=jnp.float32)
        picked += jnp.dot(other, other_ref[:, :features], preferred_element_type=jnp.float32)
        rows.append(picked.astype(jnp.bfloat16))
    rows = rows[0] if count == 1 else jnp.concatenate(rows, axis=0)
    gate = jnp.dot(rows, gate_ref[0], preferred_element_type=jnp.float32)
    upper = jnp.dot(rows, up_ref[0], preferred_element_type=jnp.float32)
    hidden = (gate / (1.0 + jnp.exp(-gate)) * upper).astype(jnp.bfloat16)
    for part, ahead in enumerate(parts):
        for b, k in enumerate(ahead):
            z = layer + k
            z = jnp.where(z >= line, z - line, z)
            for c in range(CORES):
                place = z * CORES + (core if c == 0 else 1 - core)
                at = pl.ds(pl.multiple_of(place * width, width), width)
                to = slice((b * CORES + c) * width, (b * CORES + c + 1) * width)
                result = jnp.dot(hidden, down_ref[0, :, at], preferred_element_type=jnp.float32)
                result = result.astype(jnp.bfloat16)
                for i in range(count):
                    outs[len(parts) * i + part][:, to] = result[i * capacity : (i + 1) * capacity]


def run_expert(inputs, weights, capacity, top_count, line, parts):
    count = len(inputs)
    operands = [rows for pair in inputs for rows in pair]
    _, features, hidden_width = weights[0].shape
    vmem = pl.BlockSpec(memory_space=pltpu.VMEM)
    outs = pl.pallas_call(
        functools.partial(
            expert_kernel, count=count, top_count=top_count, line=line, parts=parts
        ),
        in_specs=[vmem] * (len(operands) + 3),
        out_specs=[vmem] * (len(parts) * count),
        out_shape=[
            jax.ShapeDtypeStruct((capacity, features // line * len(ahead)), jnp.bfloat16)
            for _ in range(count)
            for ahead in parts
        ],
        compiler_params=pltpu.CompilerParams(vmem_limit_bytes=SMALL_VMEM),
        cost_estimate=pl.CostEstimate(
            flops=6 * count * capacity * features * hidden_width,
            bytes_accessed=6 * features * hidden_width + 8 * count * capacity * features,
            transcendentals=count * capacity * hidden_width,
        ),
        name="expert",
    )(*operands, *weights)
    return [outs[len(parts) * i : len(parts) * (i + 1)] for i in range(count)]


def pair_step(pool_size, j, core):
    if pool_size == 4 and j in (1, 2):
        return jnp.where(core == 0, j, 3 - j)
    return j


def combine_kernel(*refs, line, near_count, far_count):
    mine, other = refs[-2:]
    near = refs[:near_count]
    chosen = [ref[...] for ref in refs[near_count : 2 * near_count]]
    combine_part(near, chosen, mine, other, 0, line, line)
    far = refs[2 * near_count : 2 * near_count + far_count]
    chosen = [ref[...] for ref in refs[2 * near_count + far_count : -2]]
    combine_part(far, chosen, mine, other, line, 1, line)


def plan_kernel(rows_ref, *outs, features, top_count, line):
    terms = routing(rows_ref, features, top_count, 4)
    pool = lax.axis_index("pool")
    member = lax.axis_index("expert")
    layer = member // CORES
    core = member - layer * CORES
    owners = []
    for k in range(line):
        z = layer - k
        z = jnp.where(z < 0, z + line, z)
        owners.append(pool * lax.axis_size("expert") + z * CORES + core)
    for ref, matrix in zip(outs, plan(terms, owners, outs[0].shape[1], None)):
        ref[...] = matrix


def plan_far(rows, features, top_count, line, capacity):
    vmem = pl.BlockSpec(memory_space=pltpu.VMEM)
    shape = (CORES * rows.shape[0], capacity)
    return pl.pallas_call(
        functools.partial(plan_kernel, features=features, top_count=top_count, line=line),
        in_specs=[vmem],
        out_specs=[vmem] * line,
        out_shape=[jax.ShapeDtypeStruct(shape, jnp.bfloat16)] * line,
        compiler_params=pltpu.CompilerParams(vmem_limit_bytes=SMALL_VMEM),
        name="plan",
    )(rows)


def plan(terms, owners, capacity, line):
    top_count, group_rows = terms[0].shape
    row = lax.broadcasted_iota(jnp.int32, (group_rows, group_rows), 0)
    column = lax.broadcasted_iota(jnp.int32, (group_rows, group_rows), 1)
    source = row
    if line is not None:
        rows = group_rows // (CORES * line)
        place = row.astype(jnp.float32)
        c = jnp.floor((place + 0.5) * (1.0 / (line * rows)))
        z = jnp.floor((place - c * (line * rows) + 0.5) * (1.0 / rows))
        source = (place + (z * CORES + c - c * line - z) * rows).astype(jnp.int32)
    table = jnp.concatenate(terms, axis=0).astype(jnp.bfloat16)
    order = (column == source).astype(jnp.float32).astype(jnp.bfloat16)
    table = lax.dot_general(
        order, table, (((1,), (1,)), ((), ())), preferred_element_type=jnp.float32
    )
    ids = table[:, :top_count]
    route = table[:, top_count : 2 * top_count]
    for k in (2, 3):
        route = route + table[:, k * top_count : (k + 1) * top_count]
    before = (column < row).astype(jnp.float32).astype(jnp.bfloat16)
    slots = lax.broadcasted_iota(jnp.int32, (group_rows, capacity), 1)
    chosen = []
    for owner in owners:
        named = ids == owner.astype(jnp.float32)
        share = jnp.sum(jnp.where(named, route, 0.0), axis=1, keepdims=True)
        routed = jnp.max(named.astype(jnp.float32), axis=1, keepdims=True)
        mask = jnp.broadcast_to(routed, (group_rows, capacity))
        slot = jnp.dot(before, mask.astype(jnp.bfloat16), preferred_element_type=jnp.float32)
        slot = jnp.where(mask > 0.0, slot, -1.0).astype(jnp.int32)
        chosen.append(jnp.where(slot == slots, share, 0.0).astype(jnp.bfloat16))
    return chosen


def combine_part(inputs, chosen, mine, other, first, steps, line):
    capacity = inputs[0].shape[0]
    _, group_rows, width = mine.shape
    rows = group_rows // (CORES * line)
    whole_lanes = capacity % 128 == 0
    if whole_lanes:
        chosen = [jnp.concatenate(chosen, axis=1)]
    for b in range(CORES * steps):
        at = slice(b * width, (b + 1) * width)
        results = [ref[:, at] for ref in inputs]
        if whole_lanes:
            results = [jnp.concatenate(results, axis=0)]
        total = sum(
            jnp.dot(matrix, result, preferred_element_type=jnp.float32)
            for matrix, result in zip(chosen, results)
        )
        total = total.astype(jnp.bfloat16)
        for z in range(line):
            for c in range(CORES):
                source = slice((c * line + z) * rows, (c * line + z + 1) * rows)
                to = slice((z * CORES + c) * rows, (z * CORES + c + 1) * rows)
                (mine if b % CORES == 0 else other)[first + b // CORES, to, :] = total[source]


def combine(near, chosen, far, far_chosen, line):
    operands = [*near, *chosen, *far, *far_chosen]
    group_rows = chosen[0].shape[0]
    shape = (line + 1, group_rows, near[0].shape[1] // (CORES * line))
    vmem = pl.BlockSpec(memory_space=pltpu.VMEM)
    return pl.pallas_call(
        functools.partial(
            combine_kernel,
            line=line,
            near_count=len(near),
            far_count=len(far),
        ),
        in_specs=[vmem] * len(operands),
        out_specs=[vmem] * 2,
        out_shape=[jax.ShapeDtypeStruct(shape, jnp.bfloat16)] * 2,
        compiler_params=pltpu.CompilerParams(vmem_limit_bytes=FETCH_VMEM),
        cost_estimate=pl.CostEstimate(
            flops=2 * group_rows * sum(rows.size for rows in near + far),
            bytes_accessed=2 * sum(rows.size for rows in near + far),
            transcendentals=0,
        ),
        name="combine",
    )(*operands)


def add_kernel(mine_ref, other_ref, *outs):
    for k, out in enumerate(outs):
        total = mine_ref[k].astype(jnp.float32) + other_ref[k].astype(jnp.float32)
        out[...] = total.astype(jnp.bfloat16)


def add(mine, other):
    steps, group_rows, width = mine.shape
    vmem = pl.BlockSpec(memory_space=pltpu.VMEM)
    return pl.pallas_call(
        add_kernel,
        in_specs=[vmem] * 2,
        out_specs=[vmem] * steps,
        out_shape=[jax.ShapeDtypeStruct((group_rows, width), jnp.bfloat16)] * steps,
        compiler_params=pltpu.CompilerParams(vmem_limit_bytes=SMALL_VMEM),
        cost_estimate=pl.CostEstimate(
            flops=mine.size, bytes_accessed=6 * mine.size, transcendentals=0
        ),
        name="add",
    )(mine, other)


def finish_kernel(*refs):
    total = refs[0][...].astype(jnp.float32)
    for ref in refs[1:-1]:
        total = total + ref[...].astype(jnp.float32)
    refs[-1][...] = total.astype(jnp.bfloat16)


def finish(parts):
    vmem = pl.BlockSpec(memory_space=pltpu.VMEM)
    return pl.pallas_call(
        finish_kernel,
        in_specs=[vmem] * len(parts),
        out_specs=vmem,
        out_shape=jax.ShapeDtypeStruct(parts[0].shape, jnp.bfloat16),
        compiler_params=pltpu.CompilerParams(vmem_limit_bytes=SMALL_VMEM),
        name="finish",
    )(*parts)


def shards(
    queries,
    kv_cache,
    block_index,
    lengths,
    residual,
    out_weight,
    norm_gain,
    expert_ids,
    route_weights,
    gate_weight,
    up_weight,
    down_weight,
    *,
    pool_size,
    expert_size,
):
    line = expert_size // CORES
    core = lax.axis_index("expert") % CORES
    group_rows, top_count = expert_ids.shape
    experts = pool_size * expert_size * gate_weight.shape[0]
    capacity = 2 * group_rows * top_count // experts
    rows = queries.shape[0]
    width = out_weight.shape[1]

    def turn(value, k):
        pairs = [
            (z * CORES + c, (z + k) % line * CORES + c) for z in range(line) for c in range(CORES)
        ]
        return lax.ppermute(value, "expert", pairs)

    def across_cores(value):
        return lax.ppermute(value, "expert", [(e, e ^ 1) for e in range(expert_size)])

    def across_pool(value, j):
        pairs = []
        for p in range(pool_size):
            for e in range(expert_size):
                step = j
                if pool_size == 4 and j in (1, 2):
                    step = j if e % CORES == 0 else 3 - j
                pairs.append((p * expert_size + e, (p ^ step) * expert_size + e))
        return lax.ppermute(value, ("pool", "expert"), pairs)

    other_weight = across_cores(out_weight)

    parts = 2
    blocks = []
    for part in range(parts):
        prepared = None if part else (residual, norm_gain)
        attention, *prepared = attend(
            queries, kv_cache, block_index, lengths, part, parts, prepared
        )
        if prepared:
            extra = across_cores(prepared[0])
        if part + 1 < parts:
            attention, queries = lax.optimization_barrier((attention, queries))
        else:
            attention, other_weight, extra = lax.optimization_barrier(
                (attention, other_weight, extra)
            )
        blocks += [attention] + [turn(attention, k) for k in range(1, line)]

    attention, held = lax.optimization_barrier((attention, (out_weight, other_weight)))
    weight, other_weight = fetch(*held)
    message, mine_rows, give = project(
        blocks, weight, other_weight, residual, extra, parts
    )

    message, held = lax.optimization_barrier((message, (gate_weight, up_weight, down_weight)))
    weights = fetch(*held)
    blocks = [message] + [turn(message, k) for k in range(1, line)]
    taken = across_cores(give)
    routed, message = lax.optimization_barrier(((expert_ids.T, route_weights.T), message))
    lines, *chosen = routing_lines(*routed, line, pool_size - 1, capacity)
    blocks, taken, weights, lines = lax.optimization_barrier((blocks, taken, weights, lines))
    normed = normalize(blocks, lines, give, taken)
    attended = assemble(mine_rows, taken, line)

    last = pool_size - 1
    arrived = [normed] + [across_pool(normed, j) for j in range(1, last)]
    if pool_size == 4:
        arrived.append(across_pool(arrived[1], 2))
    else:
        arrived.append(across_pool(normed, last))
    crossed = [across_cores(rows) for rows in arrived[:last]]
    if pool_size == 4:
        crossed = [crossed[0], crossed[2], crossed[1]]
    pairs = list(zip(arrived[:last], crossed))
    steps = list(range(line))
    near = run_expert(pairs, weights, capacity, top_count, line, [steps])
    near = [part for (part,) in near]
    far, _ = lax.optimization_barrier((arrived[last], near))
    results = run_expert(
        [(far, across_cores(far))], weights, capacity, top_count, line, [[k] for k in steps]
    )[0]
    far_results = [turn(part, k) if k else part for k, part in enumerate(results)]
    far_chosen = plan_far(far, normed.shape[1] - ID_COLUMNS, top_count, line, capacity)
    returned = [across_pool(near[j], j) for j in range(1, last)]
    returned, far_results = lax.optimization_barrier((returned, far_results))
    returned = [near[0]] + returned
    mine, other = combine(returned, chosen, far_results, far_chosen, line)
    *summed, far_sum = add(mine, across_cores(other))
    landed = [turn(rows, k) if k else rows for k, rows in enumerate(summed)]
    final = finish(landed + [across_pool(far_sum, last)])
    return (attended, final)


def solution(mesh):
    return jax.shard_map(
        functools.partial(
            shards, pool_size=mesh.shape["pool"], expert_size=mesh.shape["expert"]
        ),
        mesh=mesh,
        in_specs=(
            P(("pool", "expert"), None),
            P(("pool", "expert"), None, None),
            P(("pool", "expert"), None),
            P(("pool", "expert")),
            P("pool", "expert"),
            P(None, "expert"),
            P("expert"),
            P("pool", None),
            P("pool", None),
            P(("pool", "expert"), None, None),
            P(("pool", "expert"), None, None),
            P(("pool", "expert"), None, None),
        ),
        out_specs=(P("pool", "expert"), P("pool", "expert")),
        check_vma=False,
    )
```

```python
import functools
import math

import jax
import jax.numpy as jnp
from jax import lax
from jax.experimental import pallas as pl
from jax.experimental.pallas import tpu as pltpu
from jax.sharding import PartitionSpec as P

HEAD_DIM = 128
CORES = 2
MASKED = -1e30
GAIN_COLUMNS = 128
TURN_ROWS = 16
ID_COLUMNS = 128
LARGE_VMEM = 60 * 2**20
SMALL_VMEM = 24 * 2**20
FETCH_VMEM = 46 * 2**20

epsilon = 1e-06


def prepare(residual_ref, gain_ref, out_ref, columns_ref):
    member = lax.axis_index("expert")
    core = member - member // CORES * CORES
    line = lax.axis_size("expert") // CORES
    rows = out_ref.shape[0] // line
    for z in range(line):
        at = pl.ds(pl.multiple_of((z * CORES + 1 - core) * rows, rows), rows)
        out_ref[z * rows : (z + 1) * rows, :] = residual_ref[at, :]
    lines = [
        term[:, at : at + GAIN_COLUMNS]
        for term in three_terms(gain_ref[...])
        for at in range(0, gain_ref.shape[1], GAIN_COLUMNS)
    ]
    lines.append(jnp.zeros((columns_ref.shape[0] - len(lines), GAIN_COLUMNS), jnp.float32))
    columns_ref[...] = jnp.concatenate(lines, axis=0).astype(jnp.bfloat16)


def attend_kernel(index_ref, length_ref, query_ref, kv_hbm, *refs, block_len, first, prepares):
    if prepares:
        residual_ref, gain_ref, out_ref, extra_ref, bias_ref, key_ref, value_ref, sems = refs
    else:
        out_ref, bias_ref, key_ref, value_ref, sems = refs
    blocks_row, rows = index_ref.shape
    positions, width = key_ref.shape
    heads = width // HEAD_DIM
    kv_half = kv_hbm.shape[1] // 2
    group_size = query_ref.shape[1] // heads // HEAD_DIM
    scale = HEAD_DIM ** (-0.5)
    base2 = scale * math.log2(math.e)
    pieces = sems.shape[1]
    copies = []
    for kind, (start, target) in enumerate(((0, key_ref), (kv_half, value_ref))):
        columns = pl.ds(start + first * HEAD_DIM, width)
        for piece in range(pieces):
            at = pl.ds(piece * (positions // pieces), positions // pieces)
            copies.append(
                pltpu.make_async_copy(
                    kv_hbm.at[at, columns], target.at[at, :], sems.at[kind, piece]
                )
            )
    for copy in copies:
        copy.start()
    if prepares:
        columns_ref = out_ref.at[:, pl.ds(query_ref.shape[1], GAIN_COLUMNS)]
        prepare(residual_ref, gain_ref, extra_ref, columns_ref)

    length = length_ref[...].astype(jnp.float32)
    high = jnp.floor(length * (1.0 / 16)) * 16.0
    pad = jnp.zeros((TURN_ROWS - blocks_row - 2, rows), jnp.float32)
    table = jnp.concatenate(
        [
            index_ref[...].astype(jnp.float32),
            high,
            length - high,
            pad,
        ],
        axis=0,
    ).astype(jnp.bfloat16)
    same = lax.broadcasted_iota(jnp.int32, (rows, rows), 0) == lax.broadcasted_iota(
        jnp.int32, (rows, rows), 1
    )
    table = lax.dot_general(
        same.astype(jnp.float32).astype(jnp.bfloat16),
        table,
        (((1,), (1,)), ((), ())),
        preferred_element_type=jnp.float32,
    )
    limit = table[:, blocks_row : blocks_row + 1] + table[:, blocks_row + 1 : blocks_row + 2]
    place = lax.broadcasted_iota(jnp.int32, (rows, positions), 1).astype(jnp.float32)
    block = jnp.floor((place + 0.5) * (1.0 / block_len))
    offset = place - block * block_len
    count = jnp.zeros((rows, positions), jnp.float32)
    for j in range(blocks_row):
        live = (table[:, j : j + 1] == block) & (offset < limit - j * block_len)
        count = count + jnp.where(live, 1.0, 0.0)
    bias_ref[...] = jnp.where(
        count > 0.0, jnp.log(jnp.maximum(count, 1.0)) * (1.0 / scale), MASKED
    )

    for g in range(heads):
        columns = [
            slice((g * group_size + h) * HEAD_DIM, (g * group_size + h + 1) * HEAD_DIM)
            for h in range(group_size)
        ]
        head = slice(g * HEAD_DIM, (g + 1) * HEAD_DIM)
        query = jnp.concatenate([query_ref[:, at] for at in columns], axis=0)
        if g == 0:
            for copy in copies[:pieces]:
                copy.wait()
        scores = lax.dot_general(
            query, key_ref[:, head], (((1,), (1,)), ((), ())), preferred_element_type=jnp.float32
        )
        scores = scores.reshape(group_size, rows, positions) + bias_ref[...][None]
        maximum = jnp.max(scores, axis=-1, keepdims=True)
        exponent = jnp.exp2((scores - maximum) * base2)
        total = jnp.sum(exponent, axis=-1, keepdims=True)
        weights = exponent.astype(jnp.bfloat16).reshape(group_size * rows, positions)
        if g == 0:
            for copy in copies[pieces:]:
                copy.wait()
        mixed = jnp.dot(weights, value_ref[:, head], preferred_element_type=jnp.float32)
        mixed = mixed.reshape(group_size, rows, HEAD_DIM) / total
        for h, at in enumerate(columns):
            out_ref[:, at] = mixed[h].astype(jnp.bfloat16)


def attend(queries, kv_cache, block_index, lengths, part, parts, prepared=None):
    rows = queries.shape[0]
    pool_blocks, block_len, kv_width = kv_cache.shape
    positions = pool_blocks * block_len
    kv_heads = kv_width // 2 // HEAD_DIM
    width = queries.shape[1] // kv_heads
    kv_flat = kv_cache.reshape(positions, kv_width)
    heads = kv_heads // parts
    first = part * heads
    operands = []
    columns = 0 if prepared is None else GAIN_COLUMNS
    out_shape = [pltpu.VMEM((rows, heads * width + columns), jnp.bfloat16)]
    if prepared is not None:
        residual, gain = prepared
        operands = [residual, gain.reshape(1, -1)]
        extra = (residual.shape[0] // CORES, residual.shape[1])
        out_shape.append(pltpu.VMEM(extra, jnp.bfloat16))
    return pl.pallas_call(
        functools.partial(
            attend_kernel, block_len=block_len, first=first, prepares=prepared is not None
        ),
        grid=(1,),
        in_specs=[
            pl.BlockSpec((block_index.shape[1], rows), lambda g: (0, 0)),
            pl.BlockSpec((1, rows), lambda g: (0, 0)),
            pl.BlockSpec((rows, heads * width), lambda g: (0, part)),
            pl.BlockSpec(memory_space=pl.ANY),
        ]
        + [pl.BlockSpec(operand.shape, lambda g: (0, 0)) for operand in operands],
        out_specs=[pl.BlockSpec(shape.shape, lambda g: (0, 0)) for shape in out_shape],
        out_shape=out_shape,
        scratch_shapes=[
            pltpu.VMEM((rows, positions), jnp.float32),
            pltpu.VMEM((positions, heads * HEAD_DIM), jnp.bfloat16),
            pltpu.VMEM((positions, heads * HEAD_DIM), jnp.bfloat16),
            pltpu.SemaphoreType.DMA((2, 2)),
        ],
        compiler_params=pltpu.CompilerParams(vmem_limit_bytes=LARGE_VMEM),
        name="attend",
    )(block_index.T, lengths.reshape(1, rows), queries, kv_flat, *operands)


def fetch_kernel(*refs, count):
    sems = refs[2 * count]
    copies = [
        pltpu.make_async_copy(refs[i], refs[count + i], sems.at[i]) for i in range(count)
    ]
    for copy in copies:
        copy.start()
    for copy in copies:
        copy.wait()


def fetch(*arrays):
    count = len(arrays)
    return pl.pallas_call(
        functools.partial(fetch_kernel, count=count),
        in_specs=[pl.BlockSpec(memory_space=pltpu.HBM)] * count,
        out_specs=[pl.BlockSpec(memory_space=pltpu.VMEM)] * count,
        out_shape=[pltpu.VMEM(array.shape, array.dtype) for array in arrays],
        scratch_shapes=[pltpu.SemaphoreType.DMA((count,))],
        compiler_params=pltpu.CompilerParams(vmem_limit_bytes=FETCH_VMEM),
        cost_estimate=pl.CostEstimate(
            flops=0, transcendentals=0, bytes_accessed=2 * sum(a.size * 2 for a in arrays)
        ),
        name="fetch",
    )(*arrays)


def project_kernel(*refs, line, parts):
    blocks = refs[: line * parts]
    (
        weight_ref,
        other_weight_ref,
        residual_ref,
        extra_ref,
        message_ref,
        mine_ref,
        give_ref,
    ) = refs[line * parts :]
    rows = blocks[0].shape[0]
    core_rows = line * rows
    width = weight_ref.shape[1]
    member = lax.axis_index("expert")
    layer = member // CORES
    core = member - layer * CORES
    depth = blocks[-1].shape[1]
    product = other_product = 0.0
    for part in range(parts):
        gathered = [ref[:, :depth] for ref in blocks[part * line : (part + 1) * line]]
        gathered = jnp.concatenate(gathered, axis=0)
        at = slice(part * depth, (part + 1) * depth)
        product += jnp.dot(gathered, weight_ref[at, :], preferred_element_type=jnp.float32)
        other_product += jnp.dot(
            gathered, other_weight_ref[at, :], preferred_element_type=jnp.float32
        )
    here = pl.ds(pl.multiple_of(core * width, width), width)
    there = pl.ds(pl.multiple_of((1 - core) * width, width), width)
    for k in range(line):
        z = layer - k
        z = jnp.where(z < 0, z + line, z)
        at = pl.ds(pl.multiple_of(z * rows, rows), rows)
        held = pl.ds(pl.multiple_of((z * CORES + core) * rows, rows), rows)
        arrived = slice(k * rows, (k + 1) * rows)
        mine = residual_ref[held, :].astype(jnp.float32) + product[arrived, :]
        mine = mine.astype(jnp.bfloat16)
        mine_ref[at, :] = mine
        message_ref[at, here] = mine
        other = extra_ref[at, :].astype(jnp.float32) + other_product[arrived, :]
        other = other.astype(jnp.bfloat16)
        give_ref[at, :] = other
        message_ref[at, there] = other
    gains = []
    pieces = width // GAIN_COLUMNS
    for k in range(line):
        lines = blocks[k][:16, depth:].astype(jnp.float32)
        for term in range(3):
            gains.append(
                jnp.concatenate(
                    [lines[term * pieces + p : term * pieces + p + 1] for p in range(pieces)], axis=1
                )
            )
    gains.append(jnp.zeros((give_ref.shape[0] - core_rows - len(gains), width), jnp.float32))
    give_ref[core_rows:, :] = jnp.concatenate(gains, axis=0).astype(jnp.bfloat16)


def project(blocks, weight, other_weight, residual, extra, parts):
    line = len(blocks) // parts
    core_rows = blocks[0].shape[0] * line
    width = weight.shape[1]
    vmem = pl.BlockSpec(memory_space=pltpu.VMEM)
    return pl.pallas_call(
        functools.partial(project_kernel, line=line, parts=parts),
        in_specs=[vmem] * (line * parts + 4),
        out_specs=[vmem] * 3,
        out_shape=[
            jax.ShapeDtypeStruct((core_rows, CORES * width), jnp.bfloat16),
            jax.ShapeDtypeStruct((core_rows, width), jnp.bfloat16),
            jax.ShapeDtypeStruct((core_rows + pl.cdiv(3 * line, 16) * 16, width), jnp.bfloat16),
        ],
        compiler_params=pltpu.CompilerParams(vmem_limit_bytes=SMALL_VMEM),
        name="project",
    )(*blocks, weight, other_weight, residual, extra)


def three_terms(value):
    terms = []
    for _ in range(3):
        terms.append(value.astype(jnp.bfloat16).astype(jnp.float32))
        value = value - terms[-1]
    return terms


def lines_kernel(ids_ref, route_ref, out_ref, *chosen, line):
    core_rows = out_ref.shape[0]
    top_count, group_rows = ids_ref.shape
    rows = group_rows // (line * CORES)
    lines = []
    terms = [ids_ref[...].astype(jnp.float32), *three_terms(route_ref[...])]
    for value in terms:
        value = jnp.concatenate(
            [
                value[:, (z * CORES + c) * rows : (z * CORES + c + 1) * rows]
                for c in range(CORES)
                for z in range(line)
            ],
            axis=1,
        )
        lines += [value[:, at : at + ID_COLUMNS] for at in range(0, group_rows, ID_COLUMNS)]
    used = top_count * len(lines)
    if used < core_rows:
        lines.append(jnp.zeros((core_rows - used, ID_COLUMNS), jnp.float32))
    out_ref[...] = jnp.concatenate(lines, axis=0).astype(jnp.bfloat16)
    pool = lax.axis_index("pool")
    member = lax.axis_index("expert")
    core = member - member // CORES * CORES
    owners = []
    for j in range(len(chosen)):
        step = pair_step(lax.axis_size("pool"), j, core)
        owners.append((pool ^ step) * lax.axis_size("expert") + member)
    for ref, matrix in zip(chosen, plan(terms, owners, chosen[0].shape[1], line)):
        ref[...] = matrix


def routing_lines(ids, route_weights, line, near_count, capacity):
    vmem = pl.BlockSpec(memory_space=pltpu.VMEM)
    return pl.pallas_call(
        functools.partial(lines_kernel, line=line),
        in_specs=[vmem] * 2,
        out_specs=[vmem] * (1 + near_count),
        out_shape=[jax.ShapeDtypeStruct((ids.shape[1] // CORES, ID_COLUMNS), jnp.bfloat16)]
        + [jax.ShapeDtypeStruct((ids.shape[1], capacity), jnp.bfloat16)] * near_count,
        compiler_params=pltpu.CompilerParams(vmem_limit_bytes=SMALL_VMEM),
        name="lines",
    )(ids, route_weights)


def normalize_kernel(lines_ref, give_ref, taken_ref, *refs):
    blocks = refs[:-1]
    out_ref = refs[-1]
    line = len(blocks)
    width = blocks[0].shape[1]
    core_rows = out_ref.shape[0]
    features = line * width
    member = lax.axis_index("expert")
    layer = member // CORES
    core = member - layer * CORES
    gains = [ref[core_rows:, :].astype(jnp.float32) for ref in (give_ref, taken_ref)]
    squares = jnp.zeros((core_rows, 1), jnp.float32)
    for block in blocks:
        attended = block[...].astype(jnp.float32)
        squares = squares + jnp.sum(attended * attended, axis=1, keepdims=True)
    inverse = lax.rsqrt(squares / features + epsilon)
    for k, block in enumerate(blocks):
        z = layer - k
        z = jnp.where(z < 0, z + line, z)
        at = pl.ds(pl.multiple_of(z * width, width), width)
        attended = block[...].astype(jnp.float32)
        mine, other = [jnp.sum(gain[3 * k : 3 * k + 3], axis=0, keepdims=True) for gain in gains]
        gain = jnp.where(
            core == 0,
            jnp.concatenate([mine, other], axis=1),
            jnp.concatenate([other, mine], axis=1),
        )
        out_ref[:, at] = (attended * inverse * gain).astype(jnp.bfloat16)

    out_ref[:, features:] = lines_ref[...]


def assemble_kernel(mine_ref, taken_ref, out_ref, *, line):
    rows = mine_ref.shape[0] // line
    member = lax.axis_index("expert")
    core = member - member // CORES * CORES
    for z in range(line):
        at = slice(z * rows, (z + 1) * rows)
        here = pl.ds(pl.multiple_of((z * CORES + core) * rows, rows), rows)
        there = pl.ds(pl.multiple_of((z * CORES + 1 - core) * rows, rows), rows)
        out_ref[here, :] = mine_ref[at, :]
        out_ref[there, :] = taken_ref[at, :]


def assemble(mine, taken, line):
    vmem = pl.BlockSpec(memory_space=pltpu.VMEM)
    return pl.pallas_call(
        functools.partial(assemble_kernel, line=line),
        in_specs=[vmem] * 2,
        out_specs=vmem,
        out_shape=jax.ShapeDtypeStruct((CORES * mine.shape[0], mine.shape[1]), mine.dtype),
        compiler_params=pltpu.CompilerParams(vmem_limit_bytes=SMALL_VMEM),
        name="assemble",
    )(mine, taken)


def normalize(blocks, lines, give, taken):
    rows, width = blocks[0].shape
    features = len(blocks) * width
    vmem = pl.BlockSpec(memory_space=pltpu.VMEM)
    return pl.pallas_call(
        normalize_kernel,
        in_specs=[vmem] * (len(blocks) + 3),
        out_specs=vmem,
        out_shape=jax.ShapeDtypeStruct((rows, features + ID_COLUMNS), jnp.bfloat16),
        compiler_params=pltpu.CompilerParams(vmem_limit_bytes=SMALL_VMEM),
        name="normalize",
    )(lines, give, taken, *blocks)


def routing(rows_ref, features, top_count, kinds):
    group_rows = CORES * rows_ref.shape[0]
    pieces = group_rows // ID_COLUMNS
    lines = rows_ref[: kinds * top_count * pieces, features:].astype(jnp.float32)
    found = []
    for kind in range(kinds):
        first = kind * pieces * top_count
        found.append(
            jnp.concatenate(
                [lines[first + p * top_count : first + (p + 1) * top_count] for p in range(pieces)],
                axis=1,
            )
        )
    return found


def expert_kernel(*refs, count, top_count, line, parts):
    inputs = [(refs[2 * i], refs[2 * i + 1]) for i in range(count)]
    gate_ref, up_ref, down_ref = refs[2 * count : 2 * count + 3]
    outs = refs[2 * count + 3 :]
    capacity = outs[0].shape[0]
    features = gate_ref.shape[1]
    width = features // (CORES * line)
    pool = lax.axis_index("pool")
    member = lax.axis_index("expert")
    layer = member // CORES
    core = member - layer * CORES
    owner = (pool * lax.axis_size("expert") + member).astype(jnp.float32)

    half = inputs[0][0].shape[0]
    group_rows = CORES * half
    before = (
        lax.broadcasted_iota(jnp.int32, (group_rows, group_rows), 0)
        < lax.broadcasted_iota(jnp.int32, (group_rows, group_rows), 1)
    ).astype(jnp.bfloat16)
    slots = lax.broadcasted_iota(jnp.int32, (capacity, group_rows), 0)
    rows = []
    for mine_ref, other_ref in inputs:
        (ids,) = routing(mine_ref, features, top_count, 1)
        routed = jnp.max((ids == owner).astype(jnp.float32), axis=0, keepdims=True)
        mask = jnp.broadcast_to(routed, (16, group_rows)).astype(jnp.bfloat16)
        slot = jnp.dot(mask, before, preferred_element_type=jnp.float32)[0:1, :]
        slot = jnp.where(routed > 0.0, slot, -1.0).astype(jnp.int32)
        chosen = (slot == slots).astype(jnp.float32)
        first, second = chosen[:, :half], chosen[:, half:]
        mine = jnp.where(core == 0, first, second).astype(jnp.bfloat16)
        other = jnp.where(core == 0, second, first).astype(jnp.bfloat16)
        picked = jnp.dot(mine, mine_ref[:, :features], preferred_element_type=jnp.float32)
        picked += jnp.dot(other, other_ref[:, :features], preferred_element_type=jnp.float32)
        rows.append(picked.astype(jnp.bfloat16))
    rows = rows[0] if count == 1 else jnp.concatenate(rows, axis=0)
    gate = jnp.dot(rows, gate_ref[0], preferred_element_type=jnp.float32)
    upper = jnp.dot(rows, up_ref[0], preferred_element_type=jnp.float32)
    hidden = (gate / (1.0 + jnp.exp(-gate)) * upper).astype(jnp.bfloat16)
    for part, ahead in enumerate(parts):
        for b, k in enumerate(ahead):
            z = layer + k
            z = jnp.where(z >= line, z - line, z)
            for c in range(CORES):
                place = z * CORES + (core if c == 0 else 1 - core)
                at = pl.ds(pl.multiple_of(place * width, width), width)
                to = slice((b * CORES + c) * width, (b * CORES + c + 1) * width)
                result = jnp.dot(hidden, down_ref[0, :, at], preferred_element_type=jnp.float32)
                result = result.astype(jnp.bfloat16)
                for i in range(count):
                    outs[len(parts) * i + part][:, to] = result[i * capacity : (i + 1) * capacity]


def run_expert(inputs, weights, capacity, top_count, line, parts):
    count = len(inputs)
    operands = [rows for pair in inputs for rows in pair]
    _, features, hidden_width = weights[0].shape
    vmem = pl.BlockSpec(memory_space=pltpu.VMEM)
    outs = pl.pallas_call(
        functools.partial(
            expert_kernel, count=count, top_count=top_count, line=line, parts=parts
        ),
        in_specs=[vmem] * (len(operands) + 3),
        out_specs=[vmem] * (len(parts) * count),
        out_shape=[
            jax.ShapeDtypeStruct((capacity, features // line * len(ahead)), jnp.bfloat16)
            for _ in range(count)
            for ahead in parts
        ],
        compiler_params=pltpu.CompilerParams(vmem_limit_bytes=SMALL_VMEM),
        cost_estimate=pl.CostEstimate(
            flops=6 * count * capacity * features * hidden_width,
            bytes_accessed=6 * features * hidden_width + 8 * count * capacity * features,
            transcendentals=count * capacity * hidden_width,
        ),
        name="expert",
    )(*operands, *weights)
    return [outs[len(parts) * i : len(parts) * (i + 1)] for i in range(count)]


def pair_step(pool_size, j, core):
    if pool_size == 4 and j in (1, 2):
        return jnp.where(core == 0, j, 3 - j)
    return j


def combine_kernel(*refs, line, near_count, far_count):
    mine, other = refs[-2:]
    near = refs[:near_count]
    chosen = [ref[...] for ref in refs[near_count : 2 * near_count]]
    combine_part(near, chosen, mine, other, 0, line, line)
    far = refs[2 * near_count : 2 * near_count + far_count]
    chosen = [ref[...] for ref in refs[2 * near_count + far_count : -2]]
    combine_part(far, chosen, mine, other, line, 1, line)


def plan_kernel(rows_ref, *outs, features, top_count, line):
    terms = routing(rows_ref, features, top_count, 4)
    pool = lax.axis_index("pool")
    member = lax.axis_index("expert")
    layer = member // CORES
    core = member - layer * CORES
    owners = []
    for k in range(line):
        z = layer - k
        z = jnp.where(z < 0, z + line, z)
        owners.append(pool * lax.axis_size("expert") + z * CORES + core)
    for ref, matrix in zip(outs, plan(terms, owners, outs[0].shape[1], None)):
        ref[...] = matrix


def plan_far(rows, features, top_count, line, capacity):
    vmem = pl.BlockSpec(memory_space=pltpu.VMEM)
    shape = (CORES * rows.shape[0], capacity)
    return pl.pallas_call(
        functools.partial(plan_kernel, features=features, top_count=top_count, line=line),
        in_specs=[vmem],
        out_specs=[vmem] * line,
        out_shape=[jax.ShapeDtypeStruct(shape, jnp.bfloat16)] * line,
        compiler_params=pltpu.CompilerParams(vmem_limit_bytes=SMALL_VMEM),
        name="plan",
    )(rows)


def plan(terms, owners, capacity, line):
    top_count, group_rows = terms[0].shape
    row = lax.broadcasted_iota(jnp.int32, (group_rows, group_rows), 0)
    column = lax.broadcasted_iota(jnp.int32, (group_rows, group_rows), 1)
    source = row
    if line is not None:
        rows = group_rows // (CORES * line)
        place = row.astype(jnp.float32)
        c = jnp.floor((place + 0.5) * (1.0 / (line * rows)))
        z = jnp.floor((place - c * (line * rows) + 0.5) * (1.0 / rows))
        source = (place + (z * CORES + c - c * line - z) * rows).astype(jnp.int32)
    table = jnp.concatenate(terms, axis=0).astype(jnp.bfloat16)
    order = (column == source).astype(jnp.float32).astype(jnp.bfloat16)
    table = lax.dot_general(
        order, table, (((1,), (1,)), ((), ())), preferred_element_type=jnp.float32
    )
    ids = table[:, :top_count]
    route = table[:, top_count : 2 * top_count]
    for k in (2, 3):
        route = route + table[:, k * top_count : (k + 1) * top_count]
    before = (column < row).astype(jnp.float32).astype(jnp.bfloat16)
    slots = lax.broadcasted_iota(jnp.int32, (group_rows, capacity), 1)
    chosen = []
    for owner in owners:
        named = ids == owner.astype(jnp.float32)
        share = jnp.sum(jnp.where(named, route, 0.0), axis=1, keepdims=True)
        routed = jnp.max(named.astype(jnp.float32), axis=1, keepdims=True)
        mask = jnp.broadcast_to(routed, (group_rows, capacity))
        slot = jnp.dot(before, mask.astype(jnp.bfloat16), preferred_element_type=jnp.float32)
        slot = jnp.where(mask > 0.0, slot, -1.0).astype(jnp.int32)
        chosen.append(jnp.where(slot == slots, share, 0.0).astype(jnp.bfloat16))
    return chosen


def combine_part(inputs, chosen, mine, other, first, steps, line):
    capacity = inputs[0].shape[0]
    _, group_rows, width = mine.shape
    rows = group_rows // (CORES * line)
    whole_lanes = capacity % 128 == 0
    if whole_lanes:
        chosen = [jnp.concatenate(chosen, axis=1)]
    for b in range(CORES * steps):
        at = slice(b * width, (b + 1) * width)
        results = [ref[:, at] for ref in inputs]
        if whole_lanes:
            results = [jnp.concatenate(results, axis=0)]
        total = sum(
            jnp.dot(matrix, result, preferred_element_type=jnp.float32)
            for matrix, result in zip(chosen, results)
        )
        total = total.astype(jnp.bfloat16)
        for z in range(line):
            for c in range(CORES):
                source = slice((c * line + z) * rows, (c * line + z + 1) * rows)
                to = slice((z * CORES + c) * rows, (z * CORES + c + 1) * rows)
                (mine if b % CORES == 0 else other)[first + b // CORES, to, :] = total[source]


def combine(near, chosen, far, far_chosen, line):
    operands = [*near, *chosen, *far, *far_chosen]
    group_rows = chosen[0].shape[0]
    shape = (line + 1, group_rows, near[0].shape[1] // (CORES * line))
    vmem = pl.BlockSpec(memory_space=pltpu.VMEM)
    return pl.pallas_call(
        functools.partial(
            combine_kernel,
            line=line,
            near_count=len(near),
            far_count=len(far),
        ),
        in_specs=[vmem] * len(operands),
        out_specs=[vmem] * 2,
        out_shape=[jax.ShapeDtypeStruct(shape, jnp.bfloat16)] * 2,
        compiler_params=pltpu.CompilerParams(vmem_limit_bytes=FETCH_VMEM),
        cost_estimate=pl.CostEstimate(
            flops=2 * group_rows * sum(rows.size for rows in near + far),
            bytes_accessed=2 * sum(rows.size for rows in near + far),
            transcendentals=0,
        ),
        name="combine",
    )(*operands)


def add_kernel(mine_ref, other_ref, *outs):
    for k, out in enumerate(outs):
        total = mine_ref[k].astype(jnp.float32) + other_ref[k].astype(jnp.float32)
        out[...] = total.astype(jnp.bfloat16)


def add(mine, other):
    steps, group_rows, width = mine.shape
    vmem = pl.BlockSpec(memory_space=pltpu.VMEM)
    return pl.pallas_call(
        add_kernel,
        in_specs=[vmem] * 2,
        out_specs=[vmem] * steps,
        out_shape=[jax.ShapeDtypeStruct((group_rows, width), jnp.bfloat16)] * steps,
        compiler_params=pltpu.CompilerParams(vmem_limit_bytes=SMALL_VMEM),
        cost_estimate=pl.CostEstimate(
            flops=mine.size, bytes_accessed=6 * mine.size, transcendentals=0
        ),
        name="add",
    )(mine, other)


def finish_kernel(*refs):
    total = refs[0][...].astype(jnp.float32)
    for ref in refs[1:-1]:
        total = total + ref[...].astype(jnp.float32)
    refs[-1][...] = total.astype(jnp.bfloat16)


def finish(parts):
    vmem = pl.BlockSpec(memory_space=pltpu.VMEM)
    return pl.pallas_call(
        finish_kernel,
        in_specs=[vmem] * len(parts),
        out_specs=vmem,
        out_shape=jax.ShapeDtypeStruct(parts[0].shape, jnp.bfloat16),
        compiler_params=pltpu.CompilerParams(vmem_limit_bytes=SMALL_VMEM),
        name="finish",
    )(*parts)


def shards(
    queries,
    kv_cache,
    block_index,
    lengths,
    residual,
    out_weight,
    norm_gain,
    expert_ids,
    route_weights,
    gate_weight,
    up_weight,
    down_weight,
    *,
    pool_size,
    expert_size,
):
    line = expert_size // CORES
    core = lax.axis_index("expert") % CORES
    group_rows, top_count = expert_ids.shape
    experts = pool_size * expert_size * gate_weight.shape[0]
    capacity = 2 * group_rows * top_count // experts
    rows = queries.shape[0]
    width = out_weight.shape[1]

    def turn(value, k):
        pairs = [
            (z * CORES + c, (z + k) % line * CORES + c) for z in range(line) for c in range(CORES)
        ]
        return lax.ppermute(value, "expert", pairs)

    def across_cores(value):
        return lax.ppermute(value, "expert", [(e, e ^ 1) for e in range(expert_size)])

    def across_pool(value, j):
        pairs = []
        for p in range(pool_size):
            for e in range(expert_size):
                step = j
                if pool_size == 4 and j in (1, 2):
                    step = j if e % CORES == 0 else 3 - j
                pairs.append((p * expert_size + e, (p ^ step) * expert_size + e))
        return lax.ppermute(value, ("pool", "expert"), pairs)

    other_weight = across_cores(out_weight)

    parts = 2
    blocks = []
    for part in range(parts):
        prepared = None if part else (residual, norm_gain)
        attention, *prepared = attend(
            queries, kv_cache, block_index, lengths, part, parts, prepared
        )
        if prepared:
            extra = across_cores(prepared[0])
        if part + 1 < parts:
            attention, queries = lax.optimization_barrier((attention, queries))
        else:
            attention, other_weight, extra = lax.optimization_barrier(
                (attention, other_weight, extra)
            )
        blocks += [attention] + [turn(attention, k) for k in range(1, line)]

    attention, held = lax.optimization_barrier((attention, (out_weight, other_weight)))
    weight, other_weight = fetch(*held)
    message, mine_rows, give = project(
        blocks, weight, other_weight, residual, extra, parts
    )

    message, held = lax.optimization_barrier((message, (gate_weight, up_weight, down_weight)))
    weights = fetch(*held)
    blocks = [message] + [turn(message, k) for k in range(1, line)]
    taken = across_cores(give)
    routed, message = lax.optimization_barrier(((expert_ids.T, route_weights.T), message))
    lines, *chosen = routing_lines(*routed, line, pool_size - 1, capacity)
    blocks, taken, weights, lines = lax.optimization_barrier((blocks, taken, weights, lines))
    normed = normalize(blocks, lines, give, taken)
    attended = assemble(mine_rows, taken, line)

    last = pool_size - 1
    arrived = [normed] + [across_pool(normed, j) for j in range(1, last)]
    if pool_size == 4:
        arrived.append(across_pool(arrived[1], 2))
    else:
        arrived.append(across_pool(normed, last))
    crossed = [across_cores(rows) for rows in arrived[:last]]
    if pool_size == 4:
        crossed = [crossed[0], crossed[2], crossed[1]]
    pairs = list(zip(arrived[:last], crossed))
    steps = list(range(line))
    near = run_expert(pairs, weights, capacity, top_count, line, [steps])
    near = [part for (part,) in near]
    far, _ = lax.optimization_barrier((arrived[last], near))
    results = run_expert(
        [(far, across_cores(far))], weights, capacity, top_count, line, [[k] for k in steps]
    )[0]
    far_results = [turn(part, k) if k else part for k, part in enumerate(results)]
    far_chosen = plan_far(far, normed.shape[1] - ID_COLUMNS, top_count, line, capacity)
    returned = [across_pool(near[j], j) for j in range(1, last)]
    returned, far_results = lax.optimization_barrier((returned, far_results))
    returned = [near[0]] + returned
    mine, other = combine(returned, chosen, far_results, far_chosen, line)
    *summed, far_sum = add(mine, across_cores(other))
    landed = [turn(rows, k) if k else rows for k, rows in enumerate(summed)]
    final = finish(landed + [across_pool(far_sum, last)])
    return (attended, final)


def solution(mesh):
    return jax.shard_map(
        functools.partial(
            shards, pool_size=mesh.shape["pool"], expert_size=mesh.shape["expert"]
        ),
        mesh=mesh,
        in_specs=(
            P(("pool", "expert"), None),
            P(("pool", "expert"), None, None),
            P(("pool", "expert"), None),
            P(("pool", "expert")),
            P("pool", "expert"),
            P(None, "expert"),
            P("expert"),
            P("pool", None),
            P("pool", None),
            P(("pool", "expert"), None, None),
            P(("pool", "expert"), None, None),
            P(("pool", "expert"), None, None),
        ),
        out_specs=(P("pool", "expert"), P("pool", "expert")),
        check_vma=False,
    )
```

```python
import functools
import math

import jax
import jax.numpy as jnp
from jax import lax
from jax.experimental import pallas as pl
from jax.experimental.pallas import tpu as pltpu
from jax.sharding import PartitionSpec as P

HEAD_DIM = 128
CORES = 2
MASKED = -1e30
GAIN_COLUMNS = 128
TURN_ROWS = 16
ID_COLUMNS = 128
LARGE_VMEM = 60 * 2**20
SMALL_VMEM = 24 * 2**20
FETCH_VMEM = 46 * 2**20

epsilon = 1e-06


def prepare(residual_ref, gain_ref, out_ref, columns_ref):
    member = lax.axis_index("expert")
    core = member - member // CORES * CORES
    line = lax.axis_size("expert") // CORES
    rows = out_ref.shape[0] // line
    for z in range(line):
        at = pl.ds(pl.multiple_of((z * CORES + 1 - core) * rows, rows), rows)
        out_ref[z * rows : (z + 1) * rows, :] = residual_ref[at, :]
    lines = [
        term[:, at : at + GAIN_COLUMNS]
        for term in three_terms(gain_ref[...])
        for at in range(0, gain_ref.shape[1], GAIN_COLUMNS)
    ]
    lines.append(jnp.zeros((columns_ref.shape[0] - len(lines), GAIN_COLUMNS), jnp.float32))
    columns_ref[...] = jnp.concatenate(lines, axis=0).astype(jnp.bfloat16)


def attend_kernel(index_ref, length_ref, query_ref, kv_hbm, *refs, block_len, first, prepares):
    if prepares:
        residual_ref, gain_ref, out_ref, extra_ref, bias_ref, key_ref, value_ref, sems = refs
    else:
        out_ref, bias_ref, key_ref, value_ref, sems = refs
    blocks_row, rows = index_ref.shape
    positions, width = key_ref.shape
    heads = width // HEAD_DIM
    kv_half = kv_hbm.shape[1] // 2
    group_size = query_ref.shape[1] // heads // HEAD_DIM
    scale = HEAD_DIM ** (-0.5)
    base2 = scale * math.log2(math.e)
    pieces = sems.shape[1]
    copies = []
    for kind, (start, target) in enumerate(((0, key_ref), (kv_half, value_ref))):
        columns = pl.ds(start + first * HEAD_DIM, width)
        for piece in range(pieces):
            at = pl.ds(piece * (positions // pieces), positions // pieces)
            copies.append(
                pltpu.make_async_copy(
                    kv_hbm.at[at, columns], target.at[at, :], sems.at[kind, piece]
                )
            )
    for copy in copies:
        copy.start()
    if prepares:
        columns_ref = out_ref.at[:, pl.ds(query_ref.shape[1], GAIN_COLUMNS)]
        prepare(residual_ref, gain_ref, extra_ref, columns_ref)

    length = length_ref[...].astype(jnp.float32)
    high = jnp.floor(length * (1.0 / 16)) * 16.0
    pad = jnp.zeros((TURN_ROWS - blocks_row - 2, rows), jnp.float32)
    table = jnp.concatenate(
        [
            index_ref[...].astype(jnp.float32),
            high,
            length - high,
            pad,
        ],
        axis=0,
    ).astype(jnp.bfloat16)
    same = lax.broadcasted_iota(jnp.int32, (rows, rows), 0) == lax.broadcasted_iota(
        jnp.int32, (rows, rows), 1
    )
    table = lax.dot_general(
        same.astype(jnp.float32).astype(jnp.bfloat16),
        table,
        (((1,), (1,)), ((), ())),
        preferred_element_type=jnp.float32,
    )
    limit = table[:, blocks_row : blocks_row + 1] + table[:, blocks_row + 1 : blocks_row + 2]
    place = lax.broadcasted_iota(jnp.int32, (rows, positions), 1).astype(jnp.float32)
    block = jnp.floor((place + 0.5) * (1.0 / block_len))
    offset = place - block * block_len
    count = jnp.zeros((rows, positions), jnp.float32)
    for j in range(blocks_row):
        live = (table[:, j : j + 1] == block) & (offset < limit - j * block_len)
        count = count + jnp.where(live, 1.0, 0.0)
    bias_ref[...] = jnp.where(
        count > 0.0, jnp.log(jnp.maximum(count, 1.0)) * (1.0 / scale), MASKED
    )

    for g in range(heads):
        columns = [
            slice((g * group_size + h) * HEAD_DIM, (g * group_size + h + 1) * HEAD_DIM)
            for h in range(group_size)
        ]
        head = slice(g * HEAD_DIM, (g + 1) * HEAD_DIM)
        query = jnp.concatenate([query_ref[:, at] for at in columns], axis=0)
        if g == 0:
            for copy in copies[:pieces]:
                copy.wait()
        scores = lax.dot_general(
            query, key_ref[:, head], (((1,), (1,)), ((), ())), preferred_element_type=jnp.float32
        )
        scores = scores.reshape(group_size, rows, positions) + bias_ref[...][None]
        maximum = jnp.max(scores, axis=-1, keepdims=True)
        exponent = jnp.exp2((scores - maximum) * base2)
        total = jnp.sum(exponent, axis=-1, keepdims=True)
        weights = exponent.astype(jnp.bfloat16).reshape(group_size * rows, positions)
        if g == 0:
            for copy in copies[pieces:]:
                copy.wait()
        mixed = jnp.dot(weights, value_ref[:, head], preferred_element_type=jnp.float32)
        mixed = mixed.reshape(group_size, rows, HEAD_DIM) / total
        for h, at in enumerate(columns):
            out_ref[:, at] = mixed[h].astype(jnp.bfloat16)


def attend(queries, kv_cache, block_index, lengths, part, parts, prepared=None):
    rows = queries.shape[0]
    pool_blocks, block_len, kv_width = kv_cache.shape
    positions = pool_blocks * block_len
    kv_heads = kv_width // 2 // HEAD_DIM
    width = queries.shape[1] // kv_heads
    kv_flat = kv_cache.reshape(positions, kv_width)
    heads = kv_heads // parts
    first = part * heads
    operands = []
    columns = 0 if prepared is None else GAIN_COLUMNS
    out_shape = [pltpu.VMEM((rows, heads * width + columns), jnp.bfloat16)]
    if prepared is not None:
        residual, gain = prepared
        operands = [residual, gain.reshape(1, -1)]
        extra = (residual.shape[0] // CORES, residual.shape[1])
        out_shape.append(pltpu.VMEM(extra, jnp.bfloat16))
    return pl.pallas_call(
        functools.partial(
            attend_kernel, block_len=block_len, first=first, prepares=prepared is not None
        ),
        grid=(1,),
        in_specs=[
            pl.BlockSpec((block_index.shape[1], rows), lambda g: (0, 0)),
            pl.BlockSpec((1, rows), lambda g: (0, 0)),
            pl.BlockSpec((rows, heads * width), lambda g: (0, part)),
            pl.BlockSpec(memory_space=pl.ANY),
        ]
        + [pl.BlockSpec(operand.shape, lambda g: (0, 0)) for operand in operands],
        out_specs=[pl.BlockSpec(shape.shape, lambda g: (0, 0)) for shape in out_shape],
        out_shape=out_shape,
        scratch_shapes=[
            pltpu.VMEM((rows, positions), jnp.float32),
            pltpu.VMEM((positions, heads * HEAD_DIM), jnp.bfloat16),
            pltpu.VMEM((positions, heads * HEAD_DIM), jnp.bfloat16),
            pltpu.SemaphoreType.DMA((2, 1)),
        ],
        compiler_params=pltpu.CompilerParams(vmem_limit_bytes=LARGE_VMEM),
        name="attend",
    )(block_index.T, lengths.reshape(1, rows), queries, kv_flat, *operands)


def fetch_kernel(*refs, count):
    sems = refs[2 * count]
    copies = [
        pltpu.make_async_copy(refs[i], refs[count + i], sems.at[i]) for i in range(count)
    ]
    for copy in copies:
        copy.start()
    for copy in copies:
        copy.wait()


def fetch(*arrays):
    count = len(arrays)
    return pl.pallas_call(
        functools.partial(fetch_kernel, count=count),
        in_specs=[pl.BlockSpec(memory_space=pltpu.HBM)] * count,
        out_specs=[pl.BlockSpec(memory_space=pltpu.VMEM)] * count,
        out_shape=[pltpu.VMEM(array.shape, array.dtype) for array in arrays],
        scratch_shapes=[pltpu.SemaphoreType.DMA((count,))],
        compiler_params=pltpu.CompilerParams(vmem_limit_bytes=FETCH_VMEM),
        cost_estimate=pl.CostEstimate(
            flops=0, transcendentals=0, bytes_accessed=2 * sum(a.size * 2 for a in arrays)
        ),
        name="fetch",
    )(*arrays)


def project_kernel(*refs, line, parts, ends):
    blocks = refs[: line * parts]
    ends_ref = refs[line * parts]
    (
        weight_ref,
        other_weight_ref,
        residual_ref,
        extra_ref,
        message_ref,
        mine_ref,
        give_ref,
    ) = refs[line * parts + ends :]
    rows = blocks[0].shape[0]
    core_rows = line * rows
    width = weight_ref.shape[1]
    member = lax.axis_index("expert")
    layer = member // CORES
    core = member - layer * CORES
    depth = blocks[-1].shape[1]

    def take(part, k):
        value = blocks[part * line + k][...]
        if ends and part == 0 and k in (1, line - 1):
            value = jnp.where(layer == (0 if k == 1 else line - 1), ends_ref[...], value)
        return value

    first = [take(0, k) for k in range(line)]
    product = other_product = 0.0
    for part in range(parts):
        gathered = [value[:, :depth] for value in first] if part == 0 else [take(part, k) for k in range(line)]
        gathered = jnp.concatenate(gathered, axis=0)
        at = slice(part * depth, (part + 1) * depth)
        product += jnp.dot(gathered, weight_ref[at, :], preferred_element_type=jnp.float32)
        other_product += jnp.dot(
            gathered, other_weight_ref[at, :], preferred_element_type=jnp.float32
        )
    here = pl.ds(pl.multiple_of(core * width, width), width)
    there = pl.ds(pl.multiple_of((1 - core) * width, width), width)
    for k in range(line):
        z = layer - k
        z = jnp.where(z < 0, z + line, z)
        at = pl.ds(pl.multiple_of(z * rows, rows), rows)
        held = pl.ds(pl.multiple_of((z * CORES + core) * rows, rows), rows)
        arrived = slice(k * rows, (k + 1) * rows)
        mine = residual_ref[held, :].astype(jnp.float32) + product[arrived, :]
        mine = mine.astype(jnp.bfloat16)
        mine_ref[at, :] = mine
        message_ref[at, here] = mine
        other = extra_ref[at, :].astype(jnp.float32) + other_product[arrived, :]
        other = other.astype(jnp.bfloat16)
        give_ref[at, :] = other
        message_ref[at, there] = other
    gains = []
    pieces = width // GAIN_COLUMNS
    for k in range(line):
        lines = first[k][:16, depth:].astype(jnp.float32)
        for term in range(3):
            gains.append(
                jnp.concatenate(
                    [lines[term * pieces + p : term * pieces + p + 1] for p in range(pieces)], axis=1
                )
            )
    gains.append(jnp.zeros((give_ref.shape[0] - core_rows - len(gains), width), jnp.float32))
    give_ref[core_rows:, :] = jnp.concatenate(gains, axis=0).astype(jnp.bfloat16)


def project(blocks, ends, weight, other_weight, residual, extra, parts):
    line = len(blocks) // parts
    core_rows = blocks[0].shape[0] * line
    width = weight.shape[1]
    vmem = pl.BlockSpec(memory_space=pltpu.VMEM)
    return pl.pallas_call(
        functools.partial(project_kernel, line=line, parts=parts, ends=len(ends)),
        in_specs=[vmem] * (line * parts + len(ends) + 4),
        out_specs=[vmem] * 3,
        out_shape=[
            jax.ShapeDtypeStruct((core_rows, CORES * width), jnp.bfloat16),
            jax.ShapeDtypeStruct((core_rows, width), jnp.bfloat16),
            jax.ShapeDtypeStruct((core_rows + pl.cdiv(3 * line, 16) * 16, width), jnp.bfloat16),
        ],
        compiler_params=pltpu.CompilerParams(vmem_limit_bytes=SMALL_VMEM),
        name="project",
    )(*blocks, *ends, weight, other_weight, residual, extra)


def three_terms(value):
    terms = []
    for _ in range(3):
        terms.append(value.astype(jnp.bfloat16).astype(jnp.float32))
        value = value - terms[-1]
    return terms


def lines_kernel(ids_ref, route_ref, out_ref, *chosen, line):
    core_rows = out_ref.shape[0]
    top_count, group_rows = ids_ref.shape
    rows = group_rows // (line * CORES)
    lines = []
    terms = [ids_ref[...].astype(jnp.float32), *three_terms(route_ref[...])]
    for value in terms:
        value = jnp.concatenate(
            [
                value[:, (z * CORES + c) * rows : (z * CORES + c + 1) * rows]
                for c in range(CORES)
                for z in range(line)
            ],
            axis=1,
        )
        lines += [value[:, at : at + ID_COLUMNS] for at in range(0, group_rows, ID_COLUMNS)]
    used = top_count * len(lines)
    if used < core_rows:
        lines.append(jnp.zeros((core_rows - used, ID_COLUMNS), jnp.float32))
    out_ref[...] = jnp.concatenate(lines, axis=0).astype(jnp.bfloat16)
    pool = lax.axis_index("pool")
    member = lax.axis_index("expert")
    core = member - member // CORES * CORES
    owners = []
    for j in range(len(chosen)):
        step = pair_step(lax.axis_size("pool"), j, core)
        owners.append((pool ^ step) * lax.axis_size("expert") + member)
    for ref, matrix in zip(chosen, plan(terms, owners, chosen[0].shape[1], line)):
        ref[...] = matrix


def routing_lines(ids, route_weights, line, near_count, capacity):
    vmem = pl.BlockSpec(memory_space=pltpu.VMEM)
    return pl.pallas_call(
        functools.partial(lines_kernel, line=line),
        in_specs=[vmem] * 2,
        out_specs=[vmem] * (1 + near_count),
        out_shape=[jax.ShapeDtypeStruct((ids.shape[1] // CORES, ID_COLUMNS), jnp.bfloat16)]
        + [jax.ShapeDtypeStruct((ids.shape[1], capacity), jnp.bfloat16)] * near_count,
        compiler_params=pltpu.CompilerParams(vmem_limit_bytes=SMALL_VMEM),
        name="lines",
    )(ids, route_weights)


def normalize_kernel(lines_ref, give_ref, taken_ref, *refs):
    blocks = refs[:-1]
    out_ref = refs[-1]
    line = len(blocks)
    width = blocks[0].shape[1]
    core_rows = out_ref.shape[0]
    features = line * width
    member = lax.axis_index("expert")
    layer = member // CORES
    core = member - layer * CORES
    gains = [ref[core_rows:, :].astype(jnp.float32) for ref in (give_ref, taken_ref)]
    squares = jnp.zeros((core_rows, 1), jnp.float32)
    for block in blocks:
        attended = block[...].astype(jnp.float32)
        squares = squares + jnp.sum(attended * attended, axis=1, keepdims=True)
    inverse = lax.rsqrt(squares / features + epsilon)
    for k, block in enumerate(blocks):
        z = layer - k
        z = jnp.where(z < 0, z + line, z)
        at = pl.ds(pl.multiple_of(z * width, width), width)
        attended = block[...].astype(jnp.float32)
        mine, other = [jnp.sum(gain[3 * k : 3 * k + 3], axis=0, keepdims=True) for gain in gains]
        gain = jnp.where(
            core == 0,
            jnp.concatenate([mine, other], axis=1),
            jnp.concatenate([other, mine], axis=1),
        )
        out_ref[:, at] = (attended * inverse * gain).astype(jnp.bfloat16)

    out_ref[:, features:] = lines_ref[...]


def assemble_kernel(mine_ref, taken_ref, out_ref, *, line):
    rows = mine_ref.shape[0] // line
    member = lax.axis_index("expert")
    core = member - member // CORES * CORES
    for z in range(line):
        at = slice(z * rows, (z + 1) * rows)
        here = pl.ds(pl.multiple_of((z * CORES + core) * rows, rows), rows)
        there = pl.ds(pl.multiple_of((z * CORES + 1 - core) * rows, rows), rows)
        out_ref[here, :] = mine_ref[at, :]
        out_ref[there, :] = taken_ref[at, :]


def assemble(mine, taken, line):
    vmem = pl.BlockSpec(memory_space=pltpu.VMEM)
    return pl.pallas_call(
        functools.partial(assemble_kernel, line=line),
        in_specs=[vmem] * 2,
        out_specs=vmem,
        out_shape=jax.ShapeDtypeStruct((CORES * mine.shape[0], mine.shape[1]), mine.dtype),
        compiler_params=pltpu.CompilerParams(vmem_limit_bytes=SMALL_VMEM),
        name="assemble",
    )(mine, taken)


def normalize(blocks, lines, give, taken):
    rows, width = blocks[0].shape
    features = len(blocks) * width
    vmem = pl.BlockSpec(memory_space=pltpu.VMEM)
    return pl.pallas_call(
        normalize_kernel,
        in_specs=[vmem] * (len(blocks) + 3),
        out_specs=vmem,
        out_shape=jax.ShapeDtypeStruct((rows, features + ID_COLUMNS), jnp.bfloat16),
        compiler_params=pltpu.CompilerParams(vmem_limit_bytes=SMALL_VMEM),
        name="normalize",
    )(lines, give, taken, *blocks)


def routing(rows_ref, features, top_count, kinds):
    group_rows = CORES * rows_ref.shape[0]
    pieces = group_rows // ID_COLUMNS
    lines = rows_ref[: kinds * top_count * pieces, features:].astype(jnp.float32)
    found = []
    for kind in range(kinds):
        first = kind * pieces * top_count
        found.append(
            jnp.concatenate(
                [lines[first + p * top_count : first + (p + 1) * top_count] for p in range(pieces)],
                axis=1,
            )
        )
    return found


def expert_kernel(*refs, count, top_count, line, parts):
    inputs = [(refs[2 * i], refs[2 * i + 1]) for i in range(count)]
    gate_ref, up_ref, down_ref = refs[2 * count : 2 * count + 3]
    outs = refs[2 * count + 3 :]
    capacity = outs[0].shape[0]
    features = gate_ref.shape[1]
    width = features // (CORES * line)
    pool = lax.axis_index("pool")
    member = lax.axis_index("expert")
    layer = member // CORES
    core = member - layer * CORES
    owner = (pool * lax.axis_size("expert") + member).astype(jnp.float32)

    half = inputs[0][0].shape[0]
    group_rows = CORES * half
    before = (
        lax.broadcasted_iota(jnp.int32, (group_rows, group_rows), 0)
        < lax.broadcasted_iota(jnp.int32, (group_rows, group_rows), 1)
    ).astype(jnp.bfloat16)
    slots = lax.broadcasted_iota(jnp.int32, (capacity, group_rows), 0)
    rows = []
    for mine_ref, other_ref in inputs:
        (ids,) = routing(mine_ref, features, top_count, 1)
        routed = jnp.max((ids == owner).astype(jnp.float32), axis=0, keepdims=True)
        mask = jnp.broadcast_to(routed, (16, group_rows)).astype(jnp.bfloat16)
        slot = jnp.dot(mask, before, preferred_element_type=jnp.float32)[0:1, :]
        slot = jnp.where(routed > 0.0, slot, -1.0).astype(jnp.int32)
        chosen = (slot == slots).astype(jnp.float32)
        first, second = chosen[:, :half], chosen[:, half:]
        mine = jnp.where(core == 0, first, second).astype(jnp.bfloat16)
        other = jnp.where(core == 0, second, first).astype(jnp.bfloat16)
        picked = jnp.dot(mine, mine_ref[:, :features], preferred_element_type=jnp.float32)
        picked += jnp.dot(other, other_ref[:, :features], preferred_element_type=jnp.float32)
        rows.append(picked.astype(jnp.bfloat16))
    rows = rows[0] if count == 1 else jnp.concatenate(rows, axis=0)
    gate = jnp.dot(rows, gate_ref[0], preferred_element_type=jnp.float32)
    upper = jnp.dot(rows, up_ref[0], preferred_element_type=jnp.float32)
    hidden = (gate / (1.0 + jnp.exp(-gate)) * upper).astype(jnp.bfloat16)
    for part, ahead in enumerate(parts):
        for b, k in enumerate(ahead):
            z = layer + k
            z = jnp.where(z >= line, z - line, z)
            for c in range(CORES):
                place = z * CORES + (core if c == 0 else 1 - core)
                at = pl.ds(pl.multiple_of(place * width, width), width)
                to = slice((b * CORES + c) * width, (b * CORES + c + 1) * width)
                result = jnp.dot(hidden, down_ref[0, :, at], preferred_element_type=jnp.float32)
                result = result.astype(jnp.bfloat16)
                for i in range(count):
                    outs[len(parts) * i + part][:, to] = result[i * capacity : (i + 1) * capacity]


def run_expert(inputs, weights, capacity, top_count, line, parts):
    count = len(inputs)
    operands = [rows for pair in inputs for rows in pair]
    _, features, hidden_width = weights[0].shape
    vmem = pl.BlockSpec(memory_space=pltpu.VMEM)
    outs = pl.pallas_call(
        functools.partial(
            expert_kernel, count=count, top_count=top_count, line=line, parts=parts
        ),
        in_specs=[vmem] * (len(operands) + 3),
        out_specs=[vmem] * (len(parts) * count),
        out_shape=[
            jax.ShapeDtypeStruct((capacity, features // line * len(ahead)), jnp.bfloat16)
            for _ in range(count)
            for ahead in parts
        ],
        compiler_params=pltpu.CompilerParams(vmem_limit_bytes=SMALL_VMEM),
        cost_estimate=pl.CostEstimate(
            flops=6 * count * capacity * features * hidden_width,
            bytes_accessed=6 * features * hidden_width + 8 * count * capacity * features,
            transcendentals=count * capacity * hidden_width,
        ),
        name="expert",
    )(*operands, *weights)
    return [outs[len(parts) * i : len(parts) * (i + 1)] for i in range(count)]


def pair_step(pool_size, j, core):
    if pool_size == 4 and j in (1, 2):
        return jnp.where(core == 0, j, 3 - j)
    return j


def combine_kernel(*refs, line, near_count, far_count):
    mine, other = refs[-2:]
    near = refs[:near_count]
    chosen = [ref[...] for ref in refs[near_count : 2 * near_count]]
    combine_part(near, chosen, mine, other, 0, line, line)
    far = refs[2 * near_count : 2 * near_count + far_count]
    chosen = [ref[...] for ref in refs[2 * near_count + far_count : -2]]
    combine_part(far, chosen, mine, other, line, 1, line)


def plan_kernel(rows_ref, *outs, features, top_count, line):
    terms = routing(rows_ref, features, top_count, 4)
    pool = lax.axis_index("pool")
    member = lax.axis_index("expert")
    layer = member // CORES
    core = member - layer * CORES
    owners = []
    for k in range(line):
        z = layer - k
        z = jnp.where(z < 0, z + line, z)
        owners.append(pool * lax.axis_size("expert") + z * CORES + core)
    for ref, matrix in zip(outs, plan(terms, owners, outs[0].shape[1], None)):
        ref[...] = matrix


def plan_far(rows, features, top_count, line, capacity):
    vmem = pl.BlockSpec(memory_space=pltpu.VMEM)
    shape = (CORES * rows.shape[0], capacity)
    return pl.pallas_call(
        functools.partial(plan_kernel, features=features, top_count=top_count, line=line),
        in_specs=[vmem],
        out_specs=[vmem] * line,
        out_shape=[jax.ShapeDtypeStruct(shape, jnp.bfloat16)] * line,
        compiler_params=pltpu.CompilerParams(vmem_limit_bytes=SMALL_VMEM),
        name="plan",
    )(rows)


def plan(terms, owners, capacity, line):
    top_count, group_rows = terms[0].shape
    row = lax.broadcasted_iota(jnp.int32, (group_rows, group_rows), 0)
    column = lax.broadcasted_iota(jnp.int32, (group_rows, group_rows), 1)
    source = row
    if line is not None:
        rows = group_rows // (CORES * line)
        place = row.astype(jnp.float32)
        c = jnp.floor((place + 0.5) * (1.0 / (line * rows)))
        z = jnp.floor((place - c * (line * rows) + 0.5) * (1.0 / rows))
        source = (place + (z * CORES + c - c * line - z) * rows).astype(jnp.int32)
    table = jnp.concatenate(terms, axis=0).astype(jnp.bfloat16)
    order = (column == source).astype(jnp.float32).astype(jnp.bfloat16)
    table = lax.dot_general(
        order, table, (((1,), (1,)), ((), ())), preferred_element_type=jnp.float32
    )
    ids = table[:, :top_count]
    route = table[:, top_count : 2 * top_count]
    for k in (2, 3):
        route = route + table[:, k * top_count : (k + 1) * top_count]
    before = (column < row).astype(jnp.float32).astype(jnp.bfloat16)
    slots = lax.broadcasted_iota(jnp.int32, (group_rows, capacity), 1)
    chosen = []
    for owner in owners:
        named = ids == owner.astype(jnp.float32)
        share = jnp.sum(jnp.where(named, route, 0.0), axis=1, keepdims=True)
        routed = jnp.max(named.astype(jnp.float32), axis=1, keepdims=True)
        mask = jnp.broadcast_to(routed, (group_rows, capacity))
        slot = jnp.dot(before, mask.astype(jnp.bfloat16), preferred_element_type=jnp.float32)
        slot = jnp.where(mask > 0.0, slot, -1.0).astype(jnp.int32)
        chosen.append(jnp.where(slot == slots, share, 0.0).astype(jnp.bfloat16))
    return chosen


def combine_part(inputs, chosen, mine, other, first, steps, line):
    capacity = inputs[0].shape[0]
    _, group_rows, width = mine.shape
    rows = group_rows // (CORES * line)
    whole_lanes = capacity % 128 == 0
    if whole_lanes:
        chosen = [jnp.concatenate(chosen, axis=1)]
    for b in range(CORES * steps):
        at = slice(b * width, (b + 1) * width)
        results = [ref[:, at] for ref in inputs]
        if whole_lanes:
            results = [jnp.concatenate(results, axis=0)]
        total = sum(
            jnp.dot(matrix, result, preferred_element_type=jnp.float32)
            for matrix, result in zip(chosen, results)
        )
        total = total.astype(jnp.bfloat16)
        for z in range(line):
            for c in range(CORES):
                source = slice((c * line + z) * rows, (c * line + z + 1) * rows)
                to = slice((z * CORES + c) * rows, (z * CORES + c + 1) * rows)
                (mine if b % CORES == 0 else other)[first + b // CORES, to, :] = total[source]


def combine(near, chosen, far, far_chosen, line):
    operands = [*near, *chosen, *far, *far_chosen]
    group_rows = chosen[0].shape[0]
    shape = (line + 1, group_rows, near[0].shape[1] // (CORES * line))
    vmem = pl.BlockSpec(memory_space=pltpu.VMEM)
    return pl.pallas_call(
        functools.partial(
            combine_kernel,
            line=line,
            near_count=len(near),
            far_count=len(far),
        ),
        in_specs=[vmem] * len(operands),
        out_specs=[vmem] * 2,
        out_shape=[jax.ShapeDtypeStruct(shape, jnp.bfloat16)] * 2,
        compiler_params=pltpu.CompilerParams(vmem_limit_bytes=FETCH_VMEM),
        cost_estimate=pl.CostEstimate(
            flops=2 * group_rows * sum(rows.size for rows in near + far),
            bytes_accessed=2 * sum(rows.size for rows in near + far),
            transcendentals=0,
        ),
        name="combine",
    )(*operands)


def add_kernel(mine_ref, other_ref, *outs):
    for k, out in enumerate(outs):
        total = mine_ref[k].astype(jnp.float32) + other_ref[k].astype(jnp.float32)
        out[...] = total.astype(jnp.bfloat16)


def add(mine, other):
    steps, group_rows, width = mine.shape
    vmem = pl.BlockSpec(memory_space=pltpu.VMEM)
    return pl.pallas_call(
        add_kernel,
        in_specs=[vmem] * 2,
        out_specs=[vmem] * steps,
        out_shape=[jax.ShapeDtypeStruct((group_rows, width), jnp.bfloat16)] * steps,
        compiler_params=pltpu.CompilerParams(vmem_limit_bytes=SMALL_VMEM),
        cost_estimate=pl.CostEstimate(
            flops=mine.size, bytes_accessed=6 * mine.size, transcendentals=0
        ),
        name="add",
    )(mine, other)


def finish_kernel(*refs):
    total = refs[0][...].astype(jnp.float32)
    for ref in refs[1:-1]:
        total = total + ref[...].astype(jnp.float32)
    refs[-1][...] = total.astype(jnp.bfloat16)


def finish(parts):
    vmem = pl.BlockSpec(memory_space=pltpu.VMEM)
    return pl.pallas_call(
        finish_kernel,
        in_specs=[vmem] * len(parts),
        out_specs=vmem,
        out_shape=jax.ShapeDtypeStruct(parts[0].shape, jnp.bfloat16),
        compiler_params=pltpu.CompilerParams(vmem_limit_bytes=SMALL_VMEM),
        name="finish",
    )(*parts)


def shards(
    queries,
    kv_cache,
    block_index,
    lengths,
    residual,
    out_weight,
    norm_gain,
    expert_ids,
    route_weights,
    gate_weight,
    up_weight,
    down_weight,
    *,
    pool_size,
    expert_size,
):
    line = expert_size // CORES
    core = lax.axis_index("expert") % CORES
    group_rows, top_count = expert_ids.shape
    experts = pool_size * expert_size * gate_weight.shape[0]
    capacity = 2 * group_rows * top_count // experts
    rows = queries.shape[0]
    width = out_weight.shape[1]

    def along_line(value, moves):
        pairs = [(a * CORES + c, b * CORES + c) for a, b in moves for c in range(CORES)]
        return lax.ppermute(value, "expert", pairs)

    def turn(value, k):
        return along_line(value, [(z, (z + k) % line) for z in range(line)])

    def across_cores(value):
        return lax.ppermute(value, "expert", [(e, e ^ 1) for e in range(expert_size)])

    def across_pool(value, j):
        pairs = []
        for p in range(pool_size):
            for e in range(expert_size):
                step = j
                if pool_size == 4 and j in (1, 2):
                    step = j if e % CORES == 0 else 3 - j
                pairs.append((p * expert_size + e, (p ^ step) * expert_size + e))
        return lax.ppermute(value, ("pool", "expert"), pairs)

    other_weight = across_cores(out_weight)

    parts = 2
    blocks = []
    for part in range(parts):
        prepared = None if part else (residual, norm_gain)
        attention, *prepared = attend(
            queries, kv_cache, block_index, lengths, part, parts, prepared
        )
        if prepared:
            extra = across_cores(prepared[0])
        if part + 1 < parts:
            attention, queries = lax.optimization_barrier((attention, queries))
        else:
            attention, other_weight, extra = lax.optimization_barrier(
                (attention, other_weight, extra)
            )
        if part == 0 and line == 4:
            far = turn(attention, 2)
            down = along_line(attention, [(0, 1), (1, 2), (2, 3)])
            up = along_line(attention, [(3, 2), (2, 1), (1, 0)])
            blocks += [attention, down, far, up]
        else:
            blocks += [attention] + [turn(attention, k) for k in range(1, line)]
    ends = []
    if line == 4:
        far, blocks[line] = lax.optimization_barrier((blocks[2], blocks[line]))
        ends = [along_line(far, [(1, 0), (2, 3)])]

    attention, held = lax.optimization_barrier((attention, (out_weight, other_weight)))
    weight, other_weight = fetch(*held)
    message, mine_rows, give = project(
        blocks, ends, weight, other_weight, residual, extra, parts
    )

    message, held = lax.optimization_barrier((message, (gate_weight, up_weight, down_weight)))
    weights = fetch(*held)
    blocks = [message] + [turn(message, k) for k in range(1, line)]
    taken = across_cores(give)
    routed, message = lax.optimization_barrier(((expert_ids.T, route_weights.T), message))
    lines, *chosen = routing_lines(*routed, line, pool_size - 1, capacity)
    blocks, taken, weights, lines = lax.optimization_barrier((blocks, taken, weights, lines))
    normed = normalize(blocks, lines, give, taken)
    attended = assemble(mine_rows, taken, line)

    last = pool_size - 1
    arrived = [normed] + [across_pool(normed, j) for j in range(1, last)]
    if pool_size == 4:
        arrived.append(across_pool(arrived[1], 2))
    else:
        arrived.append(across_pool(normed, last))
    crossed = [across_cores(rows) for rows in arrived[:last]]
    if pool_size == 4:
        crossed = [crossed[0], crossed[2], crossed[1]]
    pairs = list(zip(arrived[:last], crossed))
    steps = list(range(line))
    near = run_expert(pairs, weights, capacity, top_count, line, [steps])
    near = [part for (part,) in near]
    far, _ = lax.optimization_barrier((arrived[last], near))
    results = run_expert(
        [(far, across_cores(far))], weights, capacity, top_count, line, [[k] for k in steps]
    )[0]
    far_results = [turn(part, k) if k else part for k, part in enumerate(results)]
    far_chosen = plan_far(far, normed.shape[1] - ID_COLUMNS, top_count, line, capacity)
    returned = [across_pool(near[j], j) for j in range(1, last)]
    returned, far_results = lax.optimization_barrier((returned, far_results))
    returned = [near[0]] + returned
    mine, other = combine(returned, chosen, far_results, far_chosen, line)
    *summed, far_sum = add(mine, across_cores(other))
    landed = [turn(rows, k) if k else rows for k, rows in enumerate(summed)]
    final = finish(landed + [across_pool(far_sum, last)])
    return (attended, final)


def solution(mesh):
    return jax.shard_map(
        functools.partial(
            shards, pool_size=mesh.shape["pool"], expert_size=mesh.shape["expert"]
        ),
        mesh=mesh,
        in_specs=(
            P(("pool", "expert"), None),
            P(("pool", "expert"), None, None),
            P(("pool", "expert"), None),
            P(("pool", "expert")),
            P("pool", "expert"),
            P(None, "expert"),
            P("expert"),
            P("pool", None),
            P("pool", None),
            P(("pool", "expert"), None, None),
            P(("pool", "expert"), None, None),
            P(("pool", "expert"), None, None),
        ),
        out_specs=(P("pool", "expert"), P("pool", "expert")),
        check_vma=False,
    )
```

```python
import functools
import math

import jax
import jax.numpy as jnp
from jax import lax
from jax.experimental import pallas as pl
from jax.experimental.pallas import tpu as pltpu
from jax.sharding import PartitionSpec as P

HEAD_DIM = 128
CORES = 2
MASKED = -1e30
GAIN_COLUMNS = 128
TURN_ROWS = 16
ID_COLUMNS = 128
LARGE_VMEM = 60 * 2**20
SMALL_VMEM = 24 * 2**20
FETCH_VMEM = 46 * 2**20

epsilon = 1e-06


def line_order(line):
    return [0] + sorted(range(1, line), key=lambda k: -min(k, line - k))


def prepare(residual_ref, gain_ref, out_ref, columns_ref):
    member = lax.axis_index("expert")
    core = member - member // CORES * CORES
    line = lax.axis_size("expert") // CORES
    rows = out_ref.shape[0] // line
    for z in range(line):
        at = pl.ds(pl.multiple_of((z * CORES + 1 - core) * rows, rows), rows)
        out_ref[z * rows : (z + 1) * rows, :] = residual_ref[at, :]
    lines = [
        term[:, at : at + GAIN_COLUMNS]
        for term in three_terms(gain_ref[...])
        for at in range(0, gain_ref.shape[1], GAIN_COLUMNS)
    ]
    lines.append(jnp.zeros((columns_ref.shape[0] - len(lines), GAIN_COLUMNS), jnp.float32))
    columns_ref[...] = jnp.concatenate(lines, axis=0).astype(jnp.bfloat16)


def attend_kernel(index_ref, length_ref, query_ref, kv_hbm, *refs, block_len, first, prepares):
    if prepares:
        residual_ref, gain_ref, out_ref, extra_ref, bias_ref, key_ref, value_ref, sems = refs
    else:
        out_ref, bias_ref, key_ref, value_ref, sems = refs
    blocks_row, rows = index_ref.shape
    positions, width = key_ref.shape
    heads = width // HEAD_DIM
    kv_half = kv_hbm.shape[1] // 2
    group_size = query_ref.shape[1] // heads // HEAD_DIM
    scale = HEAD_DIM ** (-0.5)
    base2 = scale * math.log2(math.e)
    pieces = sems.shape[1]
    copies = []
    for kind, (start, target) in enumerate(((0, key_ref), (kv_half, value_ref))):
        columns = pl.ds(start + first * HEAD_DIM, width)
        for piece in range(pieces):
            at = pl.ds(piece * (positions // pieces), positions // pieces)
            copies.append(
                pltpu.make_async_copy(
                    kv_hbm.at[at, columns], target.at[at, :], sems.at[kind, piece]
                )
            )
    for copy in copies:
        copy.start()
    if prepares:
        columns_ref = out_ref.at[:, pl.ds(query_ref.shape[1], GAIN_COLUMNS)]
        prepare(residual_ref, gain_ref, extra_ref, columns_ref)

    length = length_ref[...].astype(jnp.float32)
    high = jnp.floor(length * (1.0 / 16)) * 16.0
    pad = jnp.zeros((TURN_ROWS - blocks_row - 2, rows), jnp.float32)
    table = jnp.concatenate(
        [
            index_ref[...].astype(jnp.float32),
            high,
            length - high,
            pad,
        ],
        axis=0,
    ).astype(jnp.bfloat16)
    same = lax.broadcasted_iota(jnp.int32, (rows, rows), 0) == lax.broadcasted_iota(
        jnp.int32, (rows, rows), 1
    )
    table = lax.dot_general(
        same.astype(jnp.float32).astype(jnp.bfloat16),
        table,
        (((1,), (1,)), ((), ())),
        preferred_element_type=jnp.float32,
    )
    limit = table[:, blocks_row : blocks_row + 1] + table[:, blocks_row + 1 : blocks_row + 2]
    place = lax.broadcasted_iota(jnp.int32, (rows, positions), 1).astype(jnp.float32)
    block = jnp.floor((place + 0.5) * (1.0 / block_len))
    offset = place - block * block_len
    count = jnp.zeros((rows, positions), jnp.float32)
    for j in range(blocks_row):
        live = (table[:, j : j + 1] == block) & (offset < limit - j * block_len)
        count = count + jnp.where(live, 1.0, 0.0)
    bias_ref[...] = jnp.where(
        count > 0.0, jnp.log(jnp.maximum(count, 1.0)) * (1.0 / scale), MASKED
    )

    for g in range(heads):
        columns = [
            slice((g * group_size + h) * HEAD_DIM, (g * group_size + h + 1) * HEAD_DIM)
            for h in range(group_size)
        ]
        head = slice(g * HEAD_DIM, (g + 1) * HEAD_DIM)
        query = jnp.concatenate([query_ref[:, at] for at in columns], axis=0)
        if g == 0:
            for copy in copies[:pieces]:
                copy.wait()
        scores = lax.dot_general(
            query, key_ref[:, head], (((1,), (1,)), ((), ())), preferred_element_type=jnp.float32
        )
        scores = scores.reshape(group_size, rows, positions) + bias_ref[...][None]
        maximum = jnp.max(scores, axis=-1, keepdims=True)
        exponent = jnp.exp2((scores - maximum) * base2)
        total = jnp.sum(exponent, axis=-1, keepdims=True)
        weights = exponent.astype(jnp.bfloat16).reshape(group_size * rows, positions)
        if g == 0:
            for copy in copies[pieces:]:
                copy.wait()
        mixed = jnp.dot(weights, value_ref[:, head], preferred_element_type=jnp.float32)
        mixed = mixed.reshape(group_size, rows, HEAD_DIM) / total
        for h, at in enumerate(columns):
            out_ref[:, at] = mixed[h].astype(jnp.bfloat16)


def attend(queries, kv_cache, block_index, lengths, part, parts, prepared=None):
    rows = queries.shape[0]
    pool_blocks, block_len, kv_width = kv_cache.shape
    positions = pool_blocks * block_len
    kv_heads = kv_width // 2 // HEAD_DIM
    width = queries.shape[1] // kv_heads
    kv_flat = kv_cache.reshape(positions, kv_width)
    heads = kv_heads // parts
    first = part * heads
    operands = []
    columns = 0 if prepared is None else GAIN_COLUMNS
    out_shape = [pltpu.VMEM((rows, heads * width + columns), jnp.bfloat16)]
    if prepared is not None:
        residual, gain = prepared
        operands = [residual, gain.reshape(1, -1)]
        extra = (residual.shape[0] // CORES, residual.shape[1])
        out_shape.append(pltpu.VMEM(extra, jnp.bfloat16))
    return pl.pallas_call(
        functools.partial(
            attend_kernel, block_len=block_len, first=first, prepares=prepared is not None
        ),
        grid=(1,),
        in_specs=[
            pl.BlockSpec((block_index.shape[1], rows), lambda g: (0, 0)),
            pl.BlockSpec((1, rows), lambda g: (0, 0)),
            pl.BlockSpec((rows, heads * width), lambda g: (0, part)),
            pl.BlockSpec(memory_space=pl.ANY),
        ]
        + [pl.BlockSpec(operand.shape, lambda g: (0, 0)) for operand in operands],
        out_specs=[pl.BlockSpec(shape.shape, lambda g: (0, 0)) for shape in out_shape],
        out_shape=out_shape,
        scratch_shapes=[
            pltpu.VMEM((rows, positions), jnp.float32),
            pltpu.VMEM((positions, heads * HEAD_DIM), jnp.bfloat16),
            pltpu.VMEM((positions, heads * HEAD_DIM), jnp.bfloat16),
            pltpu.SemaphoreType.DMA((2, 2)),
        ],
        compiler_params=pltpu.CompilerParams(vmem_limit_bytes=LARGE_VMEM),
        name="attend",
    )(block_index.T, lengths.reshape(1, rows), queries, kv_flat, *operands)


def fetch_kernel(*refs, count):
    sems = refs[2 * count]
    copies = [
        pltpu.make_async_copy(refs[i], refs[count + i], sems.at[i]) for i in range(count)
    ]
    for copy in copies:
        copy.start()
    for copy in copies:
        copy.wait()


def fetch(*arrays):
    count = len(arrays)
    return pl.pallas_call(
        functools.partial(fetch_kernel, count=count),
        in_specs=[pl.BlockSpec(memory_space=pltpu.HBM)] * count,
        out_specs=[pl.BlockSpec(memory_space=pltpu.VMEM)] * count,
        out_shape=[pltpu.VMEM(array.shape, array.dtype) for array in arrays],
        scratch_shapes=[pltpu.SemaphoreType.DMA((count,))],
        compiler_params=pltpu.CompilerParams(vmem_limit_bytes=FETCH_VMEM),
        cost_estimate=pl.CostEstimate(
            flops=0, transcendentals=0, bytes_accessed=2 * sum(a.size * 2 for a in arrays)
        ),
        name="fetch",
    )(*arrays)


def project_kernel(*refs, line, parts):
    blocks = refs[: line * parts]
    (
        weight_ref,
        other_weight_ref,
        residual_ref,
        extra_ref,
        message_ref,
        mine_ref,
        give_ref,
    ) = refs[line * parts :]
    rows = blocks[0].shape[0]
    core_rows = line * rows
    width = weight_ref.shape[1]
    member = lax.axis_index("expert")
    layer = member // CORES
    core = member - layer * CORES
    depth = blocks[-1].shape[1]
    product = other_product = 0.0
    for part in range(parts):
        gathered = [ref[:, :depth] for ref in blocks[part * line : (part + 1) * line]]
        gathered = jnp.concatenate(gathered, axis=0)
        at = slice(part * depth, (part + 1) * depth)
        product += jnp.dot(gathered, weight_ref[at, :], preferred_element_type=jnp.float32)
        other_product += jnp.dot(
            gathered, other_weight_ref[at, :], preferred_element_type=jnp.float32
        )
    here = pl.ds(pl.multiple_of(core * width, width), width)
    there = pl.ds(pl.multiple_of((1 - core) * width, width), width)
    for k, step in enumerate(line_order(line)):
        z = layer - step
        z = jnp.where(z < 0, z + line, z)
        at = pl.ds(pl.multiple_of(z * rows, rows), rows)
        held = pl.ds(pl.multiple_of((z * CORES + core) * rows, rows), rows)
        arrived = slice(k * rows, (k + 1) * rows)
        mine = residual_ref[held, :].astype(jnp.float32) + product[arrived, :]
        mine = mine.astype(jnp.bfloat16)
        mine_ref[at, :] = mine
        message_ref[at, here] = mine
        other = extra_ref[at, :].astype(jnp.float32) + other_product[arrived, :]
        other = other.astype(jnp.bfloat16)
        give_ref[at, :] = other
        message_ref[at, there] = other
    gains = []
    pieces = width // GAIN_COLUMNS
    for k in range(line):
        lines = blocks[k][:16, depth:].astype(jnp.float32)
        for term in range(3):
            gains.append(
                jnp.concatenate(
                    [lines[term * pieces + p : term * pieces + p + 1] for p in range(pieces)], axis=1
                )
            )
    gains.append(jnp.zeros((give_ref.shape[0] - core_rows - len(gains), width), jnp.float32))
    give_ref[core_rows:, :] = jnp.concatenate(gains, axis=0).astype(jnp.bfloat16)


def project(blocks, weight, other_weight, residual, extra, parts):
    line = len(blocks) // parts
    core_rows = blocks[0].shape[0] * line
    width = weight.shape[1]
    vmem = pl.BlockSpec(memory_space=pltpu.VMEM)
    return pl.pallas_call(
        functools.partial(project_kernel, line=line, parts=parts),
        in_specs=[vmem] * (line * parts + 4),
        out_specs=[vmem] * 3,
        out_shape=[
            jax.ShapeDtypeStruct((core_rows, CORES * width), jnp.bfloat16),
            jax.ShapeDtypeStruct((core_rows, width), jnp.bfloat16),
            jax.ShapeDtypeStruct((core_rows + pl.cdiv(3 * line, 16) * 16, width), jnp.bfloat16),
        ],
        compiler_params=pltpu.CompilerParams(vmem_limit_bytes=SMALL_VMEM),
        name="project",
    )(*blocks, weight, other_weight, residual, extra)


def three_terms(value):
    terms = []
    for _ in range(3):
        terms.append(value.astype(jnp.bfloat16).astype(jnp.float32))
        value = value - terms[-1]
    return terms


def lines_kernel(ids_ref, route_ref, out_ref, *chosen, line):
    core_rows = out_ref.shape[0]
    top_count, group_rows = ids_ref.shape
    rows = group_rows // (line * CORES)
    lines = []
    terms = [ids_ref[...].astype(jnp.float32), *three_terms(route_ref[...])]
    for value in terms:
        value = jnp.concatenate(
            [
                value[:, (z * CORES + c) * rows : (z * CORES + c + 1) * rows]
                for c in range(CORES)
                for z in range(line)
            ],
            axis=1,
        )
        lines += [value[:, at : at + ID_COLUMNS] for at in range(0, group_rows, ID_COLUMNS)]
    used = top_count * len(lines)
    if used < core_rows:
        lines.append(jnp.zeros((core_rows - used, ID_COLUMNS), jnp.float32))
    out_ref[...] = jnp.concatenate(lines, axis=0).astype(jnp.bfloat16)
    pool = lax.axis_index("pool")
    member = lax.axis_index("expert")
    core = member - member // CORES * CORES
    owners = []
    for j in range(len(chosen)):
        step = pair_step(lax.axis_size("pool"), j, core)
        owners.append((pool ^ step) * lax.axis_size("expert") + member)
    for ref, matrix in zip(chosen, plan(terms, owners, chosen[0].shape[1], line)):
        ref[...] = matrix


def routing_lines(ids, route_weights, line, near_count, capacity):
    vmem = pl.BlockSpec(memory_space=pltpu.VMEM)
    return pl.pallas_call(
        functools.partial(lines_kernel, line=line),
        in_specs=[vmem] * 2,
        out_specs=[vmem] * (1 + near_count),
        out_shape=[jax.ShapeDtypeStruct((ids.shape[1] // CORES, ID_COLUMNS), jnp.bfloat16)]
        + [jax.ShapeDtypeStruct((ids.shape[1], capacity), jnp.bfloat16)] * near_count,
        compiler_params=pltpu.CompilerParams(vmem_limit_bytes=SMALL_VMEM),
        name="lines",
    )(ids, route_weights)


def normalize_kernel(lines_ref, give_ref, taken_ref, *refs):
    blocks = refs[:-1]
    out_ref = refs[-1]
    line = len(blocks)
    width = blocks[0].shape[1]
    core_rows = out_ref.shape[0]
    features = line * width
    member = lax.axis_index("expert")
    layer = member // CORES
    core = member - layer * CORES
    gains = [ref[core_rows:, :].astype(jnp.float32) for ref in (give_ref, taken_ref)]
    squares = jnp.zeros((core_rows, 1), jnp.float32)
    for block in blocks:
        attended = block[...].astype(jnp.float32)
        squares = squares + jnp.sum(attended * attended, axis=1, keepdims=True)
    inverse = lax.rsqrt(squares / features + epsilon)
    for step, block in enumerate(blocks):
        k = line_order(line).index(step)
        z = layer - step
        z = jnp.where(z < 0, z + line, z)
        at = pl.ds(pl.multiple_of(z * width, width), width)
        attended = block[...].astype(jnp.float32)
        mine, other = [jnp.sum(gain[3 * k : 3 * k + 3], axis=0, keepdims=True) for gain in gains]
        gain = jnp.where(
            core == 0,
            jnp.concatenate([mine, other], axis=1),
            jnp.concatenate([other, mine], axis=1),
        )
        out_ref[:, at] = (attended * inverse * gain).astype(jnp.bfloat16)

    out_ref[:, features:] = lines_ref[...]


def assemble_kernel(mine_ref, taken_ref, out_ref, *, line):
    rows = mine_ref.shape[0] // line
    member = lax.axis_index("expert")
    core = member - member // CORES * CORES
    for z in range(line):
        at = slice(z * rows, (z + 1) * rows)
        here = pl.ds(pl.multiple_of((z * CORES + core) * rows, rows), rows)
        there = pl.ds(pl.multiple_of((z * CORES + 1 - core) * rows, rows), rows)
        out_ref[here, :] = mine_ref[at, :]
        out_ref[there, :] = taken_ref[at, :]


def assemble(mine, taken, line):
    vmem = pl.BlockSpec(memory_space=pltpu.VMEM)
    return pl.pallas_call(
        functools.partial(assemble_kernel, line=line),
        in_specs=[vmem] * 2,
        out_specs=vmem,
        out_shape=jax.ShapeDtypeStruct((CORES * mine.shape[0], mine.shape[1]), mine.dtype),
        compiler_params=pltpu.CompilerParams(vmem_limit_bytes=SMALL_VMEM),
        name="assemble",
    )(mine, taken)


def normalize(blocks, lines, give, taken):
    rows, width = blocks[0].shape
    features = len(blocks) * width
    vmem = pl.BlockSpec(memory_space=pltpu.VMEM)
    return pl.pallas_call(
        normalize_kernel,
        in_specs=[vmem] * (len(blocks) + 3),
        out_specs=vmem,
        out_shape=jax.ShapeDtypeStruct((rows, features + ID_COLUMNS), jnp.bfloat16),
        compiler_params=pltpu.CompilerParams(vmem_limit_bytes=SMALL_VMEM),
        name="normalize",
    )(lines, give, taken, *blocks)


def routing(rows_ref, features, top_count, kinds):
    group_rows = CORES * rows_ref.shape[0]
    pieces = group_rows // ID_COLUMNS
    lines = rows_ref[: kinds * top_count * pieces, features:].astype(jnp.float32)
    found = []
    for kind in range(kinds):
        first = kind * pieces * top_count
        found.append(
            jnp.concatenate(
                [lines[first + p * top_count : first + (p + 1) * top_count] for p in range(pieces)],
                axis=1,
            )
        )
    return found


def expert_kernel(*refs, count, top_count, line, parts):
    inputs = [(refs[2 * i], refs[2 * i + 1]) for i in range(count)]
    gate_ref, up_ref, down_ref = refs[2 * count : 2 * count + 3]
    outs = refs[2 * count + 3 :]
    capacity = outs[0].shape[0]
    features = gate_ref.shape[1]
    width = features // (CORES * line)
    pool = lax.axis_index("pool")
    member = lax.axis_index("expert")
    layer = member // CORES
    core = member - layer * CORES
    owner = (pool * lax.axis_size("expert") + member).astype(jnp.float32)

    half = inputs[0][0].shape[0]
    group_rows = CORES * half
    before = (
        lax.broadcasted_iota(jnp.int32, (group_rows, group_rows), 0)
        < lax.broadcasted_iota(jnp.int32, (group_rows, group_rows), 1)
    ).astype(jnp.bfloat16)
    slots = lax.broadcasted_iota(jnp.int32, (capacity, group_rows), 0)
    rows = []
    for mine_ref, other_ref in inputs:
        (ids,) = routing(mine_ref, features, top_count, 1)
        routed = jnp.max((ids == owner).astype(jnp.float32), axis=0, keepdims=True)
        mask = jnp.broadcast_to(routed, (16, group_rows)).astype(jnp.bfloat16)
        slot = jnp.dot(mask, before, preferred_element_type=jnp.float32)[0:1, :]
        slot = jnp.where(routed > 0.0, slot, -1.0).astype(jnp.int32)
        chosen = (slot == slots).astype(jnp.float32)
        first, second = chosen[:, :half], chosen[:, half:]
        mine = jnp.where(core == 0, first, second).astype(jnp.bfloat16)
        other = jnp.where(core == 0, second, first).astype(jnp.bfloat16)
        picked = jnp.dot(mine, mine_ref[:, :features], preferred_element_type=jnp.float32)
        picked += jnp.dot(other, other_ref[:, :features], preferred_element_type=jnp.float32)
        rows.append(picked.astype(jnp.bfloat16))
    rows = rows[0] if count == 1 else jnp.concatenate(rows, axis=0)
    gate = jnp.dot(rows, gate_ref[0], preferred_element_type=jnp.float32)
    upper = jnp.dot(rows, up_ref[0], preferred_element_type=jnp.float32)
    hidden = (gate / (1.0 + jnp.exp(-gate)) * upper).astype(jnp.bfloat16)
    for part, ahead in enumerate(parts):
        for b, k in enumerate(ahead):
            z = layer + k
            z = jnp.where(z >= line, z - line, z)
            for c in range(CORES):
                place = z * CORES + (core if c == 0 else 1 - core)
                at = pl.ds(pl.multiple_of(place * width, width), width)
                to = slice((b * CORES + c) * width, (b * CORES + c + 1) * width)
                result = jnp.dot(hidden, down_ref[0, :, at], preferred_element_type=jnp.float32)
                result = result.astype(jnp.bfloat16)
                for i in range(count):
                    outs[len(parts) * i + part][:, to] = result[i * capacity : (i + 1) * capacity]


def run_expert(inputs, weights, capacity, top_count, line, parts):
    count = len(inputs)
    operands = [rows for pair in inputs for rows in pair]
    _, features, hidden_width = weights[0].shape
    vmem = pl.BlockSpec(memory_space=pltpu.VMEM)
    outs = pl.pallas_call(
        functools.partial(
            expert_kernel, count=count, top_count=top_count, line=line, parts=parts
        ),
        in_specs=[vmem] * (len(operands) + 3),
        out_specs=[vmem] * (len(parts) * count),
        out_shape=[
            jax.ShapeDtypeStruct((capacity, features // line * len(ahead)), jnp.bfloat16)
            for _ in range(count)
            for ahead in parts
        ],
        compiler_params=pltpu.CompilerParams(vmem_limit_bytes=SMALL_VMEM),
        cost_estimate=pl.CostEstimate(
            flops=6 * count * capacity * features * hidden_width,
            bytes_accessed=6 * features * hidden_width + 8 * count * capacity * features,
            transcendentals=count * capacity * hidden_width,
        ),
        name="expert",
    )(*operands, *weights)
    return [outs[len(parts) * i : len(parts) * (i + 1)] for i in range(count)]


def pair_step(pool_size, j, core):
    if pool_size == 4 and j in (1, 2):
        return jnp.where(core == 0, j, 3 - j)
    return j


def combine_kernel(*refs, line, near_count, far_count):
    mine, other = refs[-2:]
    near = refs[:near_count]
    chosen = [ref[...] for ref in refs[near_count : 2 * near_count]]
    combine_part(near, chosen, mine, other, 0, line, line)
    far = refs[2 * near_count : 2 * near_count + far_count]
    chosen = [ref[...] for ref in refs[2 * near_count + far_count : -2]]
    combine_part(far, chosen, mine, other, line, 1, line)


def plan_kernel(rows_ref, *outs, features, top_count, line):
    terms = routing(rows_ref, features, top_count, 4)
    pool = lax.axis_index("pool")
    member = lax.axis_index("expert")
    layer = member // CORES
    core = member - layer * CORES
    owners = []
    for k in range(line):
        z = layer - k
        z = jnp.where(z < 0, z + line, z)
        owners.append(pool * lax.axis_size("expert") + z * CORES + core)
    for ref, matrix in zip(outs, plan(terms, owners, outs[0].shape[1], None)):
        ref[...] = matrix


def plan_far(rows, features, top_count, line, capacity):
    vmem = pl.BlockSpec(memory_space=pltpu.VMEM)
    shape = (CORES * rows.shape[0], capacity)
    return pl.pallas_call(
        functools.partial(plan_kernel, features=features, top_count=top_count, line=line),
        in_specs=[vmem],
        out_specs=[vmem] * line,
        out_shape=[jax.ShapeDtypeStruct(shape, jnp.bfloat16)] * line,
        compiler_params=pltpu.CompilerParams(vmem_limit_bytes=SMALL_VMEM),
        name="plan",
    )(rows)


def plan(terms, owners, capacity, line):
    top_count, group_rows = terms[0].shape
    row = lax.broadcasted_iota(jnp.int32, (group_rows, group_rows), 0)
    column = lax.broadcasted_iota(jnp.int32, (group_rows, group_rows), 1)
    source = row
    if line is not None:
        rows = group_rows // (CORES * line)
        place = row.astype(jnp.float32)
        c = jnp.floor((place + 0.5) * (1.0 / (line * rows)))
        z = jnp.floor((place - c * (line * rows) + 0.5) * (1.0 / rows))
        source = (place + (z * CORES + c - c * line - z) * rows).astype(jnp.int32)
    table = jnp.concatenate(terms, axis=0).astype(jnp.bfloat16)
    order = (column == source).astype(jnp.float32).astype(jnp.bfloat16)
    table = lax.dot_general(
        order, table, (((1,), (1,)), ((), ())), preferred_element_type=jnp.float32
    )
    ids = table[:, :top_count]
    route = table[:, top_count : 2 * top_count]
    for k in (2, 3):
        route = route + table[:, k * top_count : (k + 1) * top_count]
    before = (column < row).astype(jnp.float32).astype(jnp.bfloat16)
    slots = lax.broadcasted_iota(jnp.int32, (group_rows, capacity), 1)
    chosen = []
    for owner in owners:
        named = ids == owner.astype(jnp.float32)
        share = jnp.sum(jnp.where(named, route, 0.0), axis=1, keepdims=True)
        routed = jnp.max(named.astype(jnp.float32), axis=1, keepdims=True)
        mask = jnp.broadcast_to(routed, (group_rows, capacity))
        slot = jnp.dot(before, mask.astype(jnp.bfloat16), preferred_element_type=jnp.float32)
        slot = jnp.where(mask > 0.0, slot, -1.0).astype(jnp.int32)
        chosen.append(jnp.where(slot == slots, share, 0.0).astype(jnp.bfloat16))
    return chosen


def combine_part(inputs, chosen, mine, other, first, steps, line):
    capacity = inputs[0].shape[0]
    _, group_rows, width = mine.shape
    rows = group_rows // (CORES * line)
    whole_lanes = capacity % 128 == 0
    if whole_lanes:
        chosen = [jnp.concatenate(chosen, axis=1)]
    for b in range(CORES * steps):
        at = slice(b * width, (b + 1) * width)
        results = [ref[:, at] for ref in inputs]
        if whole_lanes:
            results = [jnp.concatenate(results, axis=0)]
        total = sum(
            jnp.dot(matrix, result, preferred_element_type=jnp.float32)
            for matrix, result in zip(chosen, results)
        )
        total = total.astype(jnp.bfloat16)
        for z in range(line):
            for c in range(CORES):
                source = slice((c * line + z) * rows, (c * line + z + 1) * rows)
                to = slice((z * CORES + c) * rows, (z * CORES + c + 1) * rows)
                (mine if b % CORES == 0 else other)[first + b // CORES, to, :] = total[source]


def combine(near, chosen, far, far_chosen, line):
    operands = [*near, *chosen, *far, *far_chosen]
    group_rows = chosen[0].shape[0]
    shape = (line + 1, group_rows, near[0].shape[1] // (CORES * line))
    vmem = pl.BlockSpec(memory_space=pltpu.VMEM)
    return pl.pallas_call(
        functools.partial(
            combine_kernel,
            line=line,
            near_count=len(near),
            far_count=len(far),
        ),
        in_specs=[vmem] * len(operands),
        out_specs=[vmem] * 2,
        out_shape=[jax.ShapeDtypeStruct(shape, jnp.bfloat16)] * 2,
        compiler_params=pltpu.CompilerParams(vmem_limit_bytes=FETCH_VMEM),
        cost_estimate=pl.CostEstimate(
            flops=2 * group_rows * sum(rows.size for rows in near + far),
            bytes_accessed=2 * sum(rows.size for rows in near + far),
            transcendentals=0,
        ),
        name="combine",
    )(*operands)


def add_kernel(mine_ref, other_ref, *outs):
    for k, out in enumerate(outs):
        total = mine_ref[k].astype(jnp.float32) + other_ref[k].astype(jnp.float32)
        out[...] = total.astype(jnp.bfloat16)


def add(mine, other):
    steps, group_rows, width = mine.shape
    vmem = pl.BlockSpec(memory_space=pltpu.VMEM)
    return pl.pallas_call(
        add_kernel,
        in_specs=[vmem] * 2,
        out_specs=[vmem] * steps,
        out_shape=[jax.ShapeDtypeStruct((group_rows, width), jnp.bfloat16)] * steps,
        compiler_params=pltpu.CompilerParams(vmem_limit_bytes=SMALL_VMEM),
        cost_estimate=pl.CostEstimate(
            flops=mine.size, bytes_accessed=6 * mine.size, transcendentals=0
        ),
        name="add",
    )(mine, other)


def finish_kernel(*refs):
    total = refs[0][...].astype(jnp.float32)
    for ref in refs[1:-1]:
        total = total + ref[...].astype(jnp.float32)
    refs[-1][...] = total.astype(jnp.bfloat16)


def finish(parts):
    vmem = pl.BlockSpec(memory_space=pltpu.VMEM)
    return pl.pallas_call(
        finish_kernel,
        in_specs=[vmem] * len(parts),
        out_specs=vmem,
        out_shape=jax.ShapeDtypeStruct(parts[0].shape, jnp.bfloat16),
        compiler_params=pltpu.CompilerParams(vmem_limit_bytes=SMALL_VMEM),
        name="finish",
    )(*parts)


def shards(
    queries,
    kv_cache,
    block_index,
    lengths,
    residual,
    out_weight,
    norm_gain,
    expert_ids,
    route_weights,
    gate_weight,
    up_weight,
    down_weight,
    *,
    pool_size,
    expert_size,
):
    line = expert_size // CORES
    core = lax.axis_index("expert") % CORES
    group_rows, top_count = expert_ids.shape
    experts = pool_size * expert_size * gate_weight.shape[0]
    capacity = 2 * group_rows * top_count // experts
    rows = queries.shape[0]
    width = out_weight.shape[1]

    def turn(value, k):
        pairs = [
            (z * CORES + c, (z + k) % line * CORES + c) for z in range(line) for c in range(CORES)
        ]
        return lax.ppermute(value, "expert", pairs)

    def turn_all(values):
        return [turn(values[k], k) if k else values[0] for k in line_order(line)]

    def across_cores(value):
        return lax.ppermute(value, "expert", [(e, e ^ 1) for e in range(expert_size)])

    def across_pool(value, j):
        pairs = []
        for p in range(pool_size):
            for e in range(expert_size):
                step = j
                if pool_size == 4 and j in (1, 2):
                    step = j if e % CORES == 0 else 3 - j
                pairs.append((p * expert_size + e, (p ^ step) * expert_size + e))
        return lax.ppermute(value, ("pool", "expert"), pairs)

    other_weight = across_cores(out_weight)

    parts = 2
    blocks = []
    for part in range(parts):
        prepared = None if part else (residual, norm_gain)
        attention, *prepared = attend(
            queries, kv_cache, block_index, lengths, part, parts, prepared
        )
        if prepared:
            extra = across_cores(prepared[0])
        if part + 1 < parts:
            attention, queries = lax.optimization_barrier((attention, queries))
        else:
            attention, other_weight, extra = lax.optimization_barrier(
                (attention, other_weight, extra)
            )
        blocks += turn_all([attention] * line)

    attention, held = lax.optimization_barrier((attention, (out_weight, other_weight)))
    weight, other_weight = fetch(*held)
    message, mine_rows, give = project(
        blocks, weight, other_weight, residual, extra, parts
    )

    message, held = lax.optimization_barrier((message, (gate_weight, up_weight, down_weight)))
    weights = fetch(*held)
    blocks = [message] + [turn(message, k) for k in range(1, line)]
    taken = across_cores(give)
    routed, message = lax.optimization_barrier(((expert_ids.T, route_weights.T), message))
    lines, *chosen = routing_lines(*routed, line, pool_size - 1, capacity)
    blocks, taken, weights, lines = lax.optimization_barrier((blocks, taken, weights, lines))
    normed = normalize(blocks, lines, give, taken)
    attended = assemble(mine_rows, taken, line)

    last = pool_size - 1
    arrived = [normed] + [across_pool(normed, j) for j in range(1, last)]
    if pool_size == 4:
        arrived.append(across_pool(arrived[1], 2))
    else:
        arrived.append(across_pool(normed, last))
    crossed = [across_cores(rows) for rows in arrived[:last]]
    if pool_size == 4:
        crossed = [crossed[0], crossed[2], crossed[1]]
    pairs = list(zip(arrived[:last], crossed))
    steps = list(range(line))
    near = run_expert(pairs, weights, capacity, top_count, line, [steps])
    near = [part for (part,) in near]
    far, _ = lax.optimization_barrier((arrived[last], near))
    results = run_expert(
        [(far, across_cores(far))], weights, capacity, top_count, line, [[k] for k in steps]
    )[0]
    far_results = turn_all(results)
    far_chosen = plan_far(far, normed.shape[1] - ID_COLUMNS, top_count, line, capacity)
    returned = [across_pool(near[j], j) for j in range(1, last)]
    returned, far_results = lax.optimization_barrier((returned, far_results))
    returned = [near[0]] + returned
    mine, other = combine(
        returned, chosen, far_results, [far_chosen[k] for k in line_order(line)], line
    )
    *summed, far_sum = add(mine, across_cores(other))
    landed = [turn(rows, k) if k else rows for k, rows in enumerate(summed)]
    final = finish(landed + [across_pool(far_sum, last)])
    return (attended, final)


def solution(mesh):
    return jax.shard_map(
        functools.partial(
            shards, pool_size=mesh.shape["pool"], expert_size=mesh.shape["expert"]
        ),
        mesh=mesh,
        in_specs=(
            P(("pool", "expert"), None),
            P(("pool", "expert"), None, None),
            P(("pool", "expert"), None),
            P(("pool", "expert")),
            P("pool", "expert"),
            P(None, "expert"),
            P("expert"),
            P("pool", None),
            P("pool", None),
            P(("pool", "expert"), None, None),
            P(("pool", "expert"), None, None),
            P(("pool", "expert"), None, None),
        ),
        out_specs=(P("pool", "expert"), P("pool", "expert")),
        check_vma=False,
    )
```

```python
import functools
import math

import jax
import jax.numpy as jnp
from jax import lax
from jax.experimental import pallas as pl
from jax.experimental.pallas import tpu as pltpu
from jax.sharding import PartitionSpec as P

HEAD_DIM = 128
CORES = 2
MASKED = -1e30
GAIN_COLUMNS = 128
TURN_ROWS = 16
ID_COLUMNS = 128
LARGE_VMEM = 60 * 2**20
SMALL_VMEM = 24 * 2**20
FETCH_VMEM = 46 * 2**20

epsilon = 1e-06


def line_order(line):
    return [0] + sorted(range(1, line), key=lambda k: -min(k, line - k))


def prepare(residual_ref, gain_ref, out_ref, columns_ref):
    member = lax.axis_index("expert")
    core = member - member // CORES * CORES
    line = lax.axis_size("expert") // CORES
    rows = out_ref.shape[0] // line
    for z in range(line):
        at = pl.ds(pl.multiple_of((z * CORES + 1 - core) * rows, rows), rows)
        out_ref[z * rows : (z + 1) * rows, :] = residual_ref[at, :]
    lines = [
        term[:, at : at + GAIN_COLUMNS]
        for term in three_terms(gain_ref[...])
        for at in range(0, gain_ref.shape[1], GAIN_COLUMNS)
    ]
    lines.append(jnp.zeros((columns_ref.shape[0] - len(lines), GAIN_COLUMNS), jnp.float32))
    columns_ref[...] = jnp.concatenate(lines, axis=0).astype(jnp.bfloat16)


def attend_kernel(index_ref, length_ref, query_ref, kv_hbm, *refs, block_len, first, prepares):
    if prepares:
        residual_ref, gain_ref, out_ref, extra_ref, bias_ref, key_ref, value_ref, sems = refs
    else:
        out_ref, bias_ref, key_ref, value_ref, sems = refs
    blocks_row, rows = index_ref.shape
    positions, width = key_ref.shape
    heads = width // HEAD_DIM
    kv_half = kv_hbm.shape[1] // 2
    group_size = query_ref.shape[1] // heads // HEAD_DIM
    scale = HEAD_DIM ** (-0.5)
    base2 = scale * math.log2(math.e)
    pieces = sems.shape[1]
    copies = []
    for kind, (start, target) in enumerate(((0, key_ref), (kv_half, value_ref))):
        columns = pl.ds(start + first * HEAD_DIM, width)
        for piece in range(pieces):
            at = pl.ds(piece * (positions // pieces), positions // pieces)
            copies.append(
                pltpu.make_async_copy(
                    kv_hbm.at[at, columns], target.at[at, :], sems.at[kind, piece]
                )
            )
    for copy in copies:
        copy.start()
    if prepares:
        columns_ref = out_ref.at[:, pl.ds(query_ref.shape[1], GAIN_COLUMNS)]
        prepare(residual_ref, gain_ref, extra_ref, columns_ref)

    length = length_ref[...].astype(jnp.float32)
    high = jnp.floor(length * (1.0 / 16)) * 16.0
    pad = jnp.zeros((TURN_ROWS - blocks_row - 2, rows), jnp.float32)
    table = jnp.concatenate(
        [
            index_ref[...].astype(jnp.float32),
            high,
            length - high,
            pad,
        ],
        axis=0,
    ).astype(jnp.bfloat16)
    same = lax.broadcasted_iota(jnp.int32, (rows, rows), 0) == lax.broadcasted_iota(
        jnp.int32, (rows, rows), 1
    )
    table = lax.dot_general(
        same.astype(jnp.float32).astype(jnp.bfloat16),
        table,
        (((1,), (1,)), ((), ())),
        preferred_element_type=jnp.float32,
    )
    limit = table[:, blocks_row : blocks_row + 1] + table[:, blocks_row + 1 : blocks_row + 2]
    place = lax.broadcasted_iota(jnp.int32, (rows, positions), 1).astype(jnp.float32)
    block = jnp.floor((place + 0.5) * (1.0 / block_len))
    offset = place - block * block_len
    count = jnp.zeros((rows, positions), jnp.float32)
    for j in range(blocks_row):
        live = (table[:, j : j + 1] == block) & (offset < limit - j * block_len)
        count = count + jnp.where(live, 1.0, 0.0)
    bias_ref[...] = jnp.where(
        count > 0.0, jnp.log(jnp.maximum(count, 1.0)) * (1.0 / scale), MASKED
    )

    for g in range(heads):
        columns = [
            slice((g * group_size + h) * HEAD_DIM, (g * group_size + h + 1) * HEAD_DIM)
            for h in range(group_size)
        ]
        head = slice(g * HEAD_DIM, (g + 1) * HEAD_DIM)
        query = jnp.concatenate([query_ref[:, at] for at in columns], axis=0)
        if g == 0:
            for copy in copies[:pieces]:
                copy.wait()
        scores = lax.dot_general(
            query, key_ref[:, head], (((1,), (1,)), ((), ())), preferred_element_type=jnp.float32
        )
        scores = scores.reshape(group_size, rows, positions) + bias_ref[...][None]
        maximum = jnp.max(scores, axis=-1, keepdims=True)
        exponent = jnp.exp2((scores - maximum) * base2)
        total = jnp.sum(exponent, axis=-1, keepdims=True)
        weights = exponent.astype(jnp.bfloat16).reshape(group_size * rows, positions)
        if g == 0:
            for copy in copies[pieces:]:
                copy.wait()
        mixed = jnp.dot(weights, value_ref[:, head], preferred_element_type=jnp.float32)
        mixed = mixed.reshape(group_size, rows, HEAD_DIM) / total
        for h, at in enumerate(columns):
            out_ref[:, at] = mixed[h].astype(jnp.bfloat16)


def attend(queries, kv_cache, block_index, lengths, part, parts, prepared=None):
    rows = queries.shape[0]
    pool_blocks, block_len, kv_width = kv_cache.shape
    positions = pool_blocks * block_len
    kv_heads = kv_width // 2 // HEAD_DIM
    width = queries.shape[1] // kv_heads
    kv_flat = kv_cache.reshape(positions, kv_width)
    heads = kv_heads // parts
    first = part * heads
    operands = []
    columns = 0 if prepared is None else GAIN_COLUMNS
    out_shape = [pltpu.VMEM((rows, heads * width + columns), jnp.bfloat16)]
    if prepared is not None:
        residual, gain = prepared
        operands = [residual, gain.reshape(1, -1)]
        extra = (residual.shape[0] // CORES, residual.shape[1])
        out_shape.append(pltpu.VMEM(extra, jnp.bfloat16))
    return pl.pallas_call(
        functools.partial(
            attend_kernel, block_len=block_len, first=first, prepares=prepared is not None
        ),
        grid=(1,),
        in_specs=[
            pl.BlockSpec((block_index.shape[1], rows), lambda g: (0, 0)),
            pl.BlockSpec((1, rows), lambda g: (0, 0)),
            pl.BlockSpec((rows, heads * width), lambda g: (0, part)),
            pl.BlockSpec(memory_space=pl.ANY),
        ]
        + [pl.BlockSpec(operand.shape, lambda g: (0, 0)) for operand in operands],
        out_specs=[pl.BlockSpec(shape.shape, lambda g: (0, 0)) for shape in out_shape],
        out_shape=out_shape,
        scratch_shapes=[
            pltpu.VMEM((rows, positions), jnp.float32),
            pltpu.VMEM((positions, heads * HEAD_DIM), jnp.bfloat16),
            pltpu.VMEM((positions, heads * HEAD_DIM), jnp.bfloat16),
            pltpu.SemaphoreType.DMA((2, 2)),
        ],
        compiler_params=pltpu.CompilerParams(vmem_limit_bytes=LARGE_VMEM),
        name="attend",
    )(block_index.T, lengths.reshape(1, rows), queries, kv_flat, *operands)


def fetch_kernel(*refs, count):
    sems = refs[2 * count]
    copies = [
        pltpu.make_async_copy(refs[i], refs[count + i], sems.at[i]) for i in range(count)
    ]
    for copy in copies:
        copy.start()
    for copy in copies:
        copy.wait()


def fetch(*arrays):
    count = len(arrays)
    return pl.pallas_call(
        functools.partial(fetch_kernel, count=count),
        in_specs=[pl.BlockSpec(memory_space=pltpu.HBM)] * count,
        out_specs=[pl.BlockSpec(memory_space=pltpu.VMEM)] * count,
        out_shape=[pltpu.VMEM(array.shape, array.dtype) for array in arrays],
        scratch_shapes=[pltpu.SemaphoreType.DMA((count,))],
        compiler_params=pltpu.CompilerParams(vmem_limit_bytes=FETCH_VMEM),
        cost_estimate=pl.CostEstimate(
            flops=0, transcendentals=0, bytes_accessed=2 * sum(a.size * 2 for a in arrays)
        ),
        name="fetch",
    )(*arrays)


def project_kernel(*refs, line, parts):
    blocks = [refs[k] for k in line_order(line)] + list(refs[line : line * parts])
    (
        weight_ref,
        other_weight_ref,
        residual_ref,
        extra_ref,
        message_ref,
        mine_ref,
        give_ref,
    ) = refs[line * parts :]
    rows = blocks[0].shape[0]
    core_rows = line * rows
    width = weight_ref.shape[1]
    member = lax.axis_index("expert")
    layer = member // CORES
    core = member - layer * CORES
    depth = blocks[-1].shape[1]
    product = other_product = 0.0
    for part in range(parts):
        gathered = [ref[:, :depth] for ref in blocks[part * line : (part + 1) * line]]
        gathered = jnp.concatenate(gathered, axis=0)
        at = slice(part * depth, (part + 1) * depth)
        product += jnp.dot(gathered, weight_ref[at, :], preferred_element_type=jnp.float32)
        other_product += jnp.dot(
            gathered, other_weight_ref[at, :], preferred_element_type=jnp.float32
        )
    here = pl.ds(pl.multiple_of(core * width, width), width)
    there = pl.ds(pl.multiple_of((1 - core) * width, width), width)
    for k, step in enumerate(line_order(line)):
        z = layer - step
        z = jnp.where(z < 0, z + line, z)
        at = pl.ds(pl.multiple_of(z * rows, rows), rows)
        held = pl.ds(pl.multiple_of((z * CORES + core) * rows, rows), rows)
        arrived = slice(k * rows, (k + 1) * rows)
        mine = residual_ref[held, :].astype(jnp.float32) + product[arrived, :]
        mine = mine.astype(jnp.bfloat16)
        mine_ref[at, :] = mine
        message_ref[at, here] = mine
        other = extra_ref[at, :].astype(jnp.float32) + other_product[arrived, :]
        other = other.astype(jnp.bfloat16)
        give_ref[at, :] = other
        message_ref[at, there] = other
    gains = []
    pieces = width // GAIN_COLUMNS
    for k in range(line):
        lines = blocks[k][:16, depth:].astype(jnp.float32)
        for term in range(3):
            gains.append(
                jnp.concatenate(
                    [lines[term * pieces + p : term * pieces + p + 1] for p in range(pieces)], axis=1
                )
            )
    gains.append(jnp.zeros((give_ref.shape[0] - core_rows - len(gains), width), jnp.float32))
    give_ref[core_rows:, :] = jnp.concatenate(gains, axis=0).astype(jnp.bfloat16)


def project(blocks, weight, other_weight, residual, extra, parts):
    line = len(blocks) // parts
    core_rows = blocks[0].shape[0] * line
    width = weight.shape[1]
    vmem = pl.BlockSpec(memory_space=pltpu.VMEM)
    return pl.pallas_call(
        functools.partial(project_kernel, line=line, parts=parts),
        in_specs=[vmem] * (line * parts + 4),
        out_specs=[vmem] * 3,
        out_shape=[
            jax.ShapeDtypeStruct((core_rows, CORES * width), jnp.bfloat16),
            jax.ShapeDtypeStruct((core_rows, width), jnp.bfloat16),
            jax.ShapeDtypeStruct((core_rows + pl.cdiv(3 * line, 16) * 16, width), jnp.bfloat16),
        ],
        compiler_params=pltpu.CompilerParams(vmem_limit_bytes=SMALL_VMEM),
        name="project",
    )(*blocks, weight, other_weight, residual, extra)


def three_terms(value):
    terms = []
    for _ in range(3):
        terms.append(value.astype(jnp.bfloat16).astype(jnp.float32))
        value = value - terms[-1]
    return terms


def lines_kernel(ids_ref, route_ref, out_ref, *chosen, line):
    core_rows = out_ref.shape[0]
    top_count, group_rows = ids_ref.shape
    rows = group_rows // (line * CORES)
    lines = []
    terms = [ids_ref[...].astype(jnp.float32), *three_terms(route_ref[...])]
    for value in terms:
        value = jnp.concatenate(
            [
                value[:, (z * CORES + c) * rows : (z * CORES + c + 1) * rows]
                for c in range(CORES)
                for z in range(line)
            ],
            axis=1,
        )
        lines += [value[:, at : at + ID_COLUMNS] for at in range(0, group_rows, ID_COLUMNS)]
    used = top_count * len(lines)
    if used < core_rows:
        lines.append(jnp.zeros((core_rows - used, ID_COLUMNS), jnp.float32))
    out_ref[...] = jnp.concatenate(lines, axis=0).astype(jnp.bfloat16)
    pool = lax.axis_index("pool")
    member = lax.axis_index("expert")
    core = member - member // CORES * CORES
    owners = []
    for j in range(len(chosen)):
        step = pair_step(lax.axis_size("pool"), j, core)
        owners.append((pool ^ step) * lax.axis_size("expert") + member)
    for ref, matrix in zip(chosen, plan(terms, owners, chosen[0].shape[1], line)):
        ref[...] = matrix


def routing_lines(ids, route_weights, line, near_count, capacity):
    vmem = pl.BlockSpec(memory_space=pltpu.VMEM)
    return pl.pallas_call(
        functools.partial(lines_kernel, line=line),
        in_specs=[vmem] * 2,
        out_specs=[vmem] * (1 + near_count),
        out_shape=[jax.ShapeDtypeStruct((ids.shape[1] // CORES, ID_COLUMNS), jnp.bfloat16)]
        + [jax.ShapeDtypeStruct((ids.shape[1], capacity), jnp.bfloat16)] * near_count,
        compiler_params=pltpu.CompilerParams(vmem_limit_bytes=SMALL_VMEM),
        name="lines",
    )(ids, route_weights)


def normalize_kernel(lines_ref, give_ref, taken_ref, *refs):
    blocks = refs[:-1]
    out_ref = refs[-1]
    line = len(blocks)
    width = blocks[0].shape[1]
    core_rows = out_ref.shape[0]
    features = line * width
    member = lax.axis_index("expert")
    layer = member // CORES
    core = member - layer * CORES
    gains = [ref[core_rows:, :].astype(jnp.float32) for ref in (give_ref, taken_ref)]
    squares = jnp.zeros((core_rows, 1), jnp.float32)
    for block in blocks:
        attended = block[...].astype(jnp.float32)
        squares = squares + jnp.sum(attended * attended, axis=1, keepdims=True)
    inverse = lax.rsqrt(squares / features + epsilon)
    for step, block in enumerate(blocks):
        k = line_order(line).index(step)
        z = layer - step
        z = jnp.where(z < 0, z + line, z)
        at = pl.ds(pl.multiple_of(z * width, width), width)
        attended = block[...].astype(jnp.float32)
        mine, other = [jnp.sum(gain[3 * k : 3 * k + 3], axis=0, keepdims=True) for gain in gains]
        gain = jnp.where(
            core == 0,
            jnp.concatenate([mine, other], axis=1),
            jnp.concatenate([other, mine], axis=1),
        )
        out_ref[:, at] = (attended * inverse * gain).astype(jnp.bfloat16)

    out_ref[:, features:] = lines_ref[...]


def assemble_kernel(mine_ref, taken_ref, out_ref, *, line):
    rows = mine_ref.shape[0] // line
    member = lax.axis_index("expert")
    core = member - member // CORES * CORES
    for z in range(line):
        at = slice(z * rows, (z + 1) * rows)
        here = pl.ds(pl.multiple_of((z * CORES + core) * rows, rows), rows)
        there = pl.ds(pl.multiple_of((z * CORES + 1 - core) * rows, rows), rows)
        out_ref[here, :] = mine_ref[at, :]
        out_ref[there, :] = taken_ref[at, :]


def assemble(mine, taken, line):
    vmem = pl.BlockSpec(memory_space=pltpu.VMEM)
    return pl.pallas_call(
        functools.partial(assemble_kernel, line=line),
        in_specs=[vmem] * 2,
        out_specs=vmem,
        out_shape=jax.ShapeDtypeStruct((CORES * mine.shape[0], mine.shape[1]), mine.dtype),
        compiler_params=pltpu.CompilerParams(vmem_limit_bytes=SMALL_VMEM),
        name="assemble",
    )(mine, taken)


def normalize(blocks, lines, give, taken):
    rows, width = blocks[0].shape
    features = len(blocks) * width
    vmem = pl.BlockSpec(memory_space=pltpu.VMEM)
    return pl.pallas_call(
        normalize_kernel,
        in_specs=[vmem] * (len(blocks) + 3),
        out_specs=vmem,
        out_shape=jax.ShapeDtypeStruct((rows, features + ID_COLUMNS), jnp.bfloat16),
        compiler_params=pltpu.CompilerParams(vmem_limit_bytes=SMALL_VMEM),
        name="normalize",
    )(lines, give, taken, *blocks)


def routing(rows_ref, features, top_count, kinds):
    group_rows = CORES * rows_ref.shape[0]
    pieces = group_rows // ID_COLUMNS
    lines = rows_ref[: kinds * top_count * pieces, features:].astype(jnp.float32)
    found = []
    for kind in range(kinds):
        first = kind * pieces * top_count
        found.append(
            jnp.concatenate(
                [lines[first + p * top_count : first + (p + 1) * top_count] for p in range(pieces)],
                axis=1,
            )
        )
    return found


def expert_kernel(*refs, count, top_count, line, parts):
    inputs = [(refs[2 * i], refs[2 * i + 1]) for i in range(count)]
    gate_ref, up_ref, down_ref = refs[2 * count : 2 * count + 3]
    outs = refs[2 * count + 3 :]
    capacity = outs[0].shape[0]
    features = gate_ref.shape[1]
    width = features // (CORES * line)
    pool = lax.axis_index("pool")
    member = lax.axis_index("expert")
    layer = member // CORES
    core = member - layer * CORES
    owner = (pool * lax.axis_size("expert") + member).astype(jnp.float32)

    half = inputs[0][0].shape[0]
    group_rows = CORES * half
    before = (
        lax.broadcasted_iota(jnp.int32, (group_rows, group_rows), 0)
        < lax.broadcasted_iota(jnp.int32, (group_rows, group_rows), 1)
    ).astype(jnp.bfloat16)
    slots = lax.broadcasted_iota(jnp.int32, (capacity, group_rows), 0)
    rows = []
    for mine_ref, other_ref in inputs:
        (ids,) = routing(mine_ref, features, top_count, 1)
        routed = jnp.max((ids == owner).astype(jnp.float32), axis=0, keepdims=True)
        mask = jnp.broadcast_to(routed, (16, group_rows)).astype(jnp.bfloat16)
        slot = jnp.dot(mask, before, preferred_element_type=jnp.float32)[0:1, :]
        slot = jnp.where(routed > 0.0, slot, -1.0).astype(jnp.int32)
        chosen = (slot == slots).astype(jnp.float32)
        first, second = chosen[:, :half], chosen[:, half:]
        mine = jnp.where(core == 0, first, second).astype(jnp.bfloat16)
        other = jnp.where(core == 0, second, first).astype(jnp.bfloat16)
        picked = jnp.dot(mine, mine_ref[:, :features], preferred_element_type=jnp.float32)
        picked += jnp.dot(other, other_ref[:, :features], preferred_element_type=jnp.float32)
        rows.append(picked.astype(jnp.bfloat16))
    rows = rows[0] if count == 1 else jnp.concatenate(rows, axis=0)
    gate = jnp.dot(rows, gate_ref[0], preferred_element_type=jnp.float32)
    upper = jnp.dot(rows, up_ref[0], preferred_element_type=jnp.float32)
    hidden = (gate / (1.0 + jnp.exp(-gate)) * upper).astype(jnp.bfloat16)
    for part, ahead in enumerate(parts):
        for b, k in enumerate(ahead):
            z = layer + k
            z = jnp.where(z >= line, z - line, z)
            for c in range(CORES):
                place = z * CORES + (core if c == 0 else 1 - core)
                at = pl.ds(pl.multiple_of(place * width, width), width)
                to = slice((b * CORES + c) * width, (b * CORES + c + 1) * width)
                result = jnp.dot(hidden, down_ref[0, :, at], preferred_element_type=jnp.float32)
                result = result.astype(jnp.bfloat16)
                for i in range(count):
                    outs[len(parts) * i + part][:, to] = result[i * capacity : (i + 1) * capacity]


def run_expert(inputs, weights, capacity, top_count, line, parts):
    count = len(inputs)
    operands = [rows for pair in inputs for rows in pair]
    _, features, hidden_width = weights[0].shape
    vmem = pl.BlockSpec(memory_space=pltpu.VMEM)
    outs = pl.pallas_call(
        functools.partial(
            expert_kernel, count=count, top_count=top_count, line=line, parts=parts
        ),
        in_specs=[vmem] * (len(operands) + 3),
        out_specs=[vmem] * (len(parts) * count),
        out_shape=[
            jax.ShapeDtypeStruct((capacity, features // line * len(ahead)), jnp.bfloat16)
            for _ in range(count)
            for ahead in parts
        ],
        compiler_params=pltpu.CompilerParams(vmem_limit_bytes=SMALL_VMEM),
        cost_estimate=pl.CostEstimate(
            flops=6 * count * capacity * features * hidden_width,
            bytes_accessed=6 * features * hidden_width + 8 * count * capacity * features,
            transcendentals=count * capacity * hidden_width,
        ),
        name="expert",
    )(*operands, *weights)
    return [outs[len(parts) * i : len(parts) * (i + 1)] for i in range(count)]


def pair_step(pool_size, j, core):
    if pool_size == 4 and j in (1, 2):
        return jnp.where(core == 0, j, 3 - j)
    return j


def combine_kernel(*refs, line, near_count, far_count):
    mine, other = refs[-2:]
    near = refs[:near_count]
    chosen = [ref[...] for ref in refs[near_count : 2 * near_count]]
    combine_part(near, chosen, mine, other, 0, line, line)
    far = refs[2 * near_count : 2 * near_count + far_count]
    chosen = [ref[...] for ref in refs[2 * near_count + far_count : -2]]
    combine_part(far, chosen, mine, other, line, 1, line)


def plan_kernel(rows_ref, *outs, features, top_count, line):
    terms = routing(rows_ref, features, top_count, 4)
    pool = lax.axis_index("pool")
    member = lax.axis_index("expert")
    layer = member // CORES
    core = member - layer * CORES
    owners = []
    for k in range(line):
        z = layer - k
        z = jnp.where(z < 0, z + line, z)
        owners.append(pool * lax.axis_size("expert") + z * CORES + core)
    for ref, matrix in zip(outs, plan(terms, owners, outs[0].shape[1], None)):
        ref[...] = matrix


def plan_far(rows, features, top_count, line, capacity):
    vmem = pl.BlockSpec(memory_space=pltpu.VMEM)
    shape = (CORES * rows.shape[0], capacity)
    return pl.pallas_call(
        functools.partial(plan_kernel, features=features, top_count=top_count, line=line),
        in_specs=[vmem],
        out_specs=[vmem] * line,
        out_shape=[jax.ShapeDtypeStruct(shape, jnp.bfloat16)] * line,
        compiler_params=pltpu.CompilerParams(vmem_limit_bytes=SMALL_VMEM),
        name="plan",
    )(rows)


def plan(terms, owners, capacity, line):
    top_count, group_rows = terms[0].shape
    row = lax.broadcasted_iota(jnp.int32, (group_rows, group_rows), 0)
    column = lax.broadcasted_iota(jnp.int32, (group_rows, group_rows), 1)
    source = row
    if line is not None:
        rows = group_rows // (CORES * line)
        place = row.astype(jnp.float32)
        c = jnp.floor((place + 0.5) * (1.0 / (line * rows)))
        z = jnp.floor((place - c * (line * rows) + 0.5) * (1.0 / rows))
        source = (place + (z * CORES + c - c * line - z) * rows).astype(jnp.int32)
    table = jnp.concatenate(terms, axis=0).astype(jnp.bfloat16)
    order = (column == source).astype(jnp.float32).astype(jnp.bfloat16)
    table = lax.dot_general(
        order, table, (((1,), (1,)), ((), ())), preferred_element_type=jnp.float32
    )
    ids = table[:, :top_count]
    route = table[:, top_count : 2 * top_count]
    for k in (2, 3):
        route = route + table[:, k * top_count : (k + 1) * top_count]
    before = (column < row).astype(jnp.float32).astype(jnp.bfloat16)
    slots = lax.broadcasted_iota(jnp.int32, (group_rows, capacity), 1)
    chosen = []
    for owner in owners:
        named = ids == owner.astype(jnp.float32)
        share = jnp.sum(jnp.where(named, route, 0.0), axis=1, keepdims=True)
        routed = jnp.max(named.astype(jnp.float32), axis=1, keepdims=True)
        mask = jnp.broadcast_to(routed, (group_rows, capacity))
        slot = jnp.dot(before, mask.astype(jnp.bfloat16), preferred_element_type=jnp.float32)
        slot = jnp.where(mask > 0.0, slot, -1.0).astype(jnp.int32)
        chosen.append(jnp.where(slot == slots, share, 0.0).astype(jnp.bfloat16))
    return chosen


def combine_part(inputs, chosen, mine, other, first, steps, line):
    capacity = inputs[0].shape[0]
    _, group_rows, width = mine.shape
    rows = group_rows // (CORES * line)
    whole_lanes = capacity % 128 == 0
    if whole_lanes:
        chosen = [jnp.concatenate(chosen, axis=1)]
    for b in range(CORES * steps):
        at = slice(b * width, (b + 1) * width)
        results = [ref[:, at] for ref in inputs]
        if whole_lanes:
            results = [jnp.concatenate(results, axis=0)]
        total = sum(
            jnp.dot(matrix, result, preferred_element_type=jnp.float32)
            for matrix, result in zip(chosen, results)
        )
        total = total.astype(jnp.bfloat16)
        for z in range(line):
            for c in range(CORES):
                source = slice((c * line + z) * rows, (c * line + z + 1) * rows)
                to = slice((z * CORES + c) * rows, (z * CORES + c + 1) * rows)
                (mine if b % CORES == 0 else other)[first + b // CORES, to, :] = total[source]


def combine(near, chosen, far, far_chosen, line):
    operands = [*near, *chosen, *far, *far_chosen]
    group_rows = chosen[0].shape[0]
    shape = (line + 1, group_rows, near[0].shape[1] // (CORES * line))
    vmem = pl.BlockSpec(memory_space=pltpu.VMEM)
    return pl.pallas_call(
        functools.partial(
            combine_kernel,
            line=line,
            near_count=len(near),
            far_count=len(far),
        ),
        in_specs=[vmem] * len(operands),
        out_specs=[vmem] * 2,
        out_shape=[jax.ShapeDtypeStruct(shape, jnp.bfloat16)] * 2,
        compiler_params=pltpu.CompilerParams(vmem_limit_bytes=FETCH_VMEM),
        cost_estimate=pl.CostEstimate(
            flops=2 * group_rows * sum(rows.size for rows in near + far),
            bytes_accessed=2 * sum(rows.size for rows in near + far),
            transcendentals=0,
        ),
        name="combine",
    )(*operands)


def add_kernel(mine_ref, other_ref, *outs):
    for k, out in enumerate(outs):
        total = mine_ref[k].astype(jnp.float32) + other_ref[k].astype(jnp.float32)
        out[...] = total.astype(jnp.bfloat16)


def add(mine, other):
    steps, group_rows, width = mine.shape
    vmem = pl.BlockSpec(memory_space=pltpu.VMEM)
    return pl.pallas_call(
        add_kernel,
        in_specs=[vmem] * 2,
        out_specs=[vmem] * steps,
        out_shape=[jax.ShapeDtypeStruct((group_rows, width), jnp.bfloat16)] * steps,
        compiler_params=pltpu.CompilerParams(vmem_limit_bytes=SMALL_VMEM),
        cost_estimate=pl.CostEstimate(
            flops=mine.size, bytes_accessed=6 * mine.size, transcendentals=0
        ),
        name="add",
    )(mine, other)


def finish_kernel(*refs):
    total = refs[0][...].astype(jnp.float32)
    for ref in refs[1:-1]:
        total = total + ref[...].astype(jnp.float32)
    refs[-1][...] = total.astype(jnp.bfloat16)


def finish(parts):
    vmem = pl.BlockSpec(memory_space=pltpu.VMEM)
    return pl.pallas_call(
        finish_kernel,
        in_specs=[vmem] * len(parts),
        out_specs=vmem,
        out_shape=jax.ShapeDtypeStruct(parts[0].shape, jnp.bfloat16),
        compiler_params=pltpu.CompilerParams(vmem_limit_bytes=SMALL_VMEM),
        name="finish",
    )(*parts)


def shards(
    queries,
    kv_cache,
    block_index,
    lengths,
    residual,
    out_weight,
    norm_gain,
    expert_ids,
    route_weights,
    gate_weight,
    up_weight,
    down_weight,
    *,
    pool_size,
    expert_size,
):
    line = expert_size // CORES
    core = lax.axis_index("expert") % CORES
    group_rows, top_count = expert_ids.shape
    experts = pool_size * expert_size * gate_weight.shape[0]
    capacity = 2 * group_rows * top_count // experts
    rows = queries.shape[0]
    width = out_weight.shape[1]

    def turn(value, k):
        pairs = [
            (z * CORES + c, (z + k) % line * CORES + c) for z in range(line) for c in range(CORES)
        ]
        return lax.ppermute(value, "expert", pairs)

    def turn_all(values):
        return [turn(values[k], k) if k else values[0] for k in line_order(line)]

    def across_cores(value):
        return lax.ppermute(value, "expert", [(e, e ^ 1) for e in range(expert_size)])

    def across_pool(value, j):
        pairs = []
        for p in range(pool_size):
            for e in range(expert_size):
                step = j
                if pool_size == 4 and j in (1, 2):
                    step = j if e % CORES == 0 else 3 - j
                pairs.append((p * expert_size + e, (p ^ step) * expert_size + e))
        return lax.ppermute(value, ("pool", "expert"), pairs)

    other_weight = across_cores(out_weight)

    parts = 2
    blocks = []
    for part in range(parts):
        prepared = None if part else (residual, norm_gain)
        attention, *prepared = attend(
            queries, kv_cache, block_index, lengths, part, parts, prepared
        )
        if prepared:
            extra = across_cores(prepared[0])
        if part + 1 < parts:
            attention, queries = lax.optimization_barrier((attention, queries))
        else:
            attention, other_weight, extra = lax.optimization_barrier(
                (attention, other_weight, extra)
            )
        if part == 0:
            blocks += [attention] + [turn(attention, k) for k in range(1, line)]
        else:
            blocks += turn_all([attention] * line)

    attention, held = lax.optimization_barrier((attention, (out_weight, other_weight)))
    weight, other_weight = fetch(*held)
    message, mine_rows, give = project(
        blocks, weight, other_weight, residual, extra, parts
    )

    message, held = lax.optimization_barrier((message, (gate_weight, up_weight, down_weight)))
    weights = fetch(*held)
    blocks = [message] + [turn(message, k) for k in range(1, line)]
    taken = across_cores(give)
    routed, message = lax.optimization_barrier(((expert_ids.T, route_weights.T), message))
    lines, *chosen = routing_lines(*routed, line, pool_size - 1, capacity)
    blocks, taken, weights, lines = lax.optimization_barrier((blocks, taken, weights, lines))
    normed = normalize(blocks, lines, give, taken)
    attended = assemble(mine_rows, taken, line)

    last = pool_size - 1
    arrived = [normed] + [across_pool(normed, j) for j in range(1, last)]
    if pool_size == 4:
        arrived.append(across_pool(arrived[1], 2))
    else:
        arrived.append(across_pool(normed, last))
    crossed = [across_cores(rows) for rows in arrived[:last]]
    if pool_size == 4:
        crossed = [crossed[0], crossed[2], crossed[1]]
    pairs = list(zip(arrived[:last], crossed))
    steps = list(range(line))
    near = run_expert(pairs, weights, capacity, top_count, line, [steps])
    near = [part for (part,) in near]
    far, _ = lax.optimization_barrier((arrived[last], near))
    results = run_expert(
        [(far, across_cores(far))], weights, capacity, top_count, line, [[k] for k in steps]
    )[0]
    far_results = turn_all(results)
    far_chosen = plan_far(far, normed.shape[1] - ID_COLUMNS, top_count, line, capacity)
    returned = [across_pool(near[j], j) for j in range(1, last)]
    returned, far_results = lax.optimization_barrier((returned, far_results))
    returned = [near[0]] + returned
    mine, other = combine(
        returned, chosen, far_results, [far_chosen[k] for k in line_order(line)], line
    )
    *summed, far_sum = add(mine, across_cores(other))
    landed = [turn(rows, k) if k else rows for k, rows in enumerate(summed)]
    final = finish(landed + [across_pool(far_sum, last)])
    return (attended, final)


def solution(mesh):
    return jax.shard_map(
        functools.partial(
            shards, pool_size=mesh.shape["pool"], expert_size=mesh.shape["expert"]
        ),
        mesh=mesh,
        in_specs=(
            P(("pool", "expert"), None),
            P(("pool", "expert"), None, None),
            P(("pool", "expert"), None),
            P(("pool", "expert")),
            P("pool", "expert"),
            P(None, "expert"),
            P("expert"),
            P("pool", None),
            P("pool", None),
            P(("pool", "expert"), None, None),
            P(("pool", "expert"), None, None),
            P(("pool", "expert"), None, None),
        ),
        out_specs=(P("pool", "expert"), P("pool", "expert")),
        check_vma=False,
    )
```
